32 devices in a mesh: shard: 4 (over y, core), ctx: 4 (over z), tensor: 2 (over x).
Axes of the slice: x: 2, y: 2, z: 4, core: 2. Of those that a mesh axis runs over, the one named last changes fastest.
Arguments:
- tokens: bfloat16 [4, 2048, 960], P('shard', ('ctx', 'tensor')), may hold values from -6 to 6
- cotangent: bfloat16 [4, 2048, 960], P('shard', ('ctx', 'tensor')), may hold values from -6 to 6
- prenorm_scaling: float32 [960], P('shard'), may hold values from 0.25 to 1.75
- hidden_gain: float32 [960], P('shard'), may hold values from 0.25 to 1.75
- query_weight: bfloat16 [960, 960], P('shard'), may hold values from -0.1875 to 0.1875
- key_matrix: bfloat16 [960, 320], P('shard'), may hold values from -0.1875 to 0.1875
- value_matrix: bfloat16 [960, 320], P('shard'), may hold values from -0.1875 to 0.1875
- output_weight: bfloat16 [960, 960], P('shard'), may hold values from -1.5 to 1.5
- gate_weight: bfloat16 [960, 2560], P('shard', 'tensor'), may hold values from -0.1875 to 0.1875
- up_weight: bfloat16 [960, 2560], P('shard', 'tensor'), may hold values from -0.1875 to 0.1875
- down_weight: bfloat16 [2560, 960], P('tensor', 'shard'), may hold values from -0.3125 to 0.3125
Outputs:
- output: bfloat16 [4, 2048, 960], P('shard', ('ctx', 'tensor'))
- input_grad: float32 [4, 2048, 960], P('shard', ('ctx', 'tensor'))
- attention_gain_grad: float32 [960], P('shard')
- hidden_gain_grad: float32 [960], P('shard')
- query_weight_grad: float32 [960, 960], P('shard')
- key_weight_grad: float32 [960, 320], P('shard')
- value_weight_grad: float32 [960, 320], P('shard')
- output_weight_grad: float32 [960, 960], P('shard')
- gate_weight_grad: float32 [960, 2560], P('shard', 'tensor')
- up_weight_grad: float32 [960, 2560], P('shard', 'tensor')
- down_weight_grad: float32 [2560, 960], P('tensor', 'shard')
The draws below stay inside these ranges and needn't reach their ends.
All inputs are finite; a program needn't handle non-finite values.
Results may differ from the reference program's by a relative error of at most 0.039.
Values may be sent and summed in bfloat16 or wider, within the bound.
No kernel may reach another device: no remote copies, remote signals or barrier semaphores. Data moves between devices by JAX's collectives and lax.ppermute only.
A program may use at most 128 MiB of HBM per device.

```python
import math
import jax
import jax.numpy as jnp
from jax import lax

MODEL_WIDTH = 960
QUERY_HEADS = 15
SHARED_KV_UNITS = 5
ATTN_UNIT_DIM = 64
FF = 2560
SEQ_LEN = 2048
SEQS = 4


def block_levels(key, extent, pieces, least, top_value):
    gain, own = 1.0, jax.random.fold_in(key, 6)
    for dim, parts in pieces:
        draws = jnp.exp(jax.random.uniform(jax.random.fold_in(own, dim), (parts,), jnp.float32, least / len(pieces), top_value / len(pieces)))
        gain = gain * jnp.repeat(draws, extent[dim] // parts).reshape([-1 if axis == dim else 1 for axis in range(len(extent))])
    return gain


def bell_draw(stream_key, dims, width, most, cuts=(), kind=jnp.bfloat16):
    array = jax.random.normal(stream_key, dims, jnp.float32) * width
    if len(cuts) > 0:
        array = block_levels(stream_key, dims, cuts, -0.22, 0.18) * array
    return jnp.clip(array, min=-most, max=most).astype(kind)


def setup_inputs(seed: int = 0) -> dict:
    key_list = jax.random.split(jax.random.key(seed), 12)
    return {
        "tokens": bell_draw(key_list[0], (SEQS, SEQ_LEN, MODEL_WIDTH), 1.0, 6.0, ((0, 4), (1, 8))),
        "cotangent": bell_draw(key_list[1], (SEQS, SEQ_LEN, MODEL_WIDTH), 1.0, 6.0, ((0, 4), (1, 8))),
        "prenorm_scaling": jnp.clip(1.0 + 0.15 * jax.random.normal(key_list[2], (MODEL_WIDTH,), jnp.float32), 0.25, 1.75),
        "hidden_gain": jnp.clip(1.0 + 0.15 * jax.random.normal(key_list[3], (MODEL_WIDTH,), jnp.float32), 0.25, 1.75),
        "query_weight": bell_draw(key_list[4], (MODEL_WIDTH, QUERY_HEADS * ATTN_UNIT_DIM), MODEL_WIDTH ** -0.5, 0.1875, ((0, 4),)),
        "key_matrix": bell_draw(key_list[5], (MODEL_WIDTH, SHARED_KV_UNITS * ATTN_UNIT_DIM), MODEL_WIDTH ** -0.5, 0.1875, ((0, 4),)),
        "value_matrix": bell_draw(key_list[6], (MODEL_WIDTH, SHARED_KV_UNITS * ATTN_UNIT_DIM), MODEL_WIDTH ** -0.5, 0.1875, ((0, 4),)),
        "output_weight": bell_draw(key_list[7], (QUERY_HEADS * ATTN_UNIT_DIM, MODEL_WIDTH), (ATTN_UNIT_DIM // 4) ** -0.5, 1.5, ((0, 4),)),
        "gate_weight": bell_draw(key_list[8], (MODEL_WIDTH, FF), MODEL_WIDTH ** -0.5, 0.1875, ((0, 4), (1, 2))),
        "up_weight": bell_draw(key_list[9], (MODEL_WIDTH, FF), MODEL_WIDTH ** -0.5, 0.1875, ((0, 4), (1, 2))),
        "down_weight": bell_draw(key_list[10], (FF, MODEL_WIDTH), (FF // 8) ** -0.5, 0.3125, ((0, 2), (1, 4))),
    }


EPS = 1e-05
THETA = 100000.0

@jax.custom_vjp
def low(v):
    return lax.optimization_barrier(v.astype(jnp.bfloat16)).astype(jnp.float32)

@jax.custom_vjp
def low_back(v):
    return v

def low_keep(v):
    return (low(v), None)

def low_pass(kept, grad):
    return (grad,)

def back_keep(v):
    return (v, None)

def back_low(kept, grad):
    return (low(grad),)
low.defvjp(low_keep, low_pass)
low_back.defvjp(back_keep, back_low)

def matmul(left, right):
    return jnp.dot(left, right, precision=lax.Precision.HIGHEST, preferred_element_type=jnp.float32)

def rotary_tables(positions, model_width):
    half_width = model_width // 2
    freqs = THETA ** (-(jnp.arange(half_width, dtype=jnp.float32) * 2.0 / model_width))
    angles = positions.astype(jnp.float32)[:, None] * freqs[None, :]
    return (jnp.cos(angles), jnp.sin(angles))

def apply_rotation(value_rows, cosine_table, sine_table):
    half_width = value_rows.shape[-1] // 2
    former = value_rows[..., :half_width]
    latter = value_rows[..., half_width:]
    cos_rows = cosine_table[:, None, :]
    sin_rows = sine_table[:, None, :]
    return jnp.concatenate([former * cos_rows - latter * sin_rows, latter * cos_rows + former * sin_rows], -1)

def attention(query_rows, key_rows, value_rows):
    series_extent = query_rows.shape[0]
    group_count = QUERY_HEADS // SHARED_KV_UNITS
    rows_per_block = math.gcd(series_extent, 512)
    block_count = series_extent // rows_per_block
    block_list = query_rows.reshape(block_count, rows_per_block, SHARED_KV_UNITS, group_count, ATTN_UNIT_DIM)
    key_pos = jnp.arange(series_extent).astype(jnp.int32)

    def one_block(pair):
        block_q, index = pair
        query_pos = (index * rows_per_block + jnp.arange(rows_per_block)).astype(jnp.int32)
        scores = jnp.einsum('qhgd,khd->hgqk', block_q, key_rows, precision=lax.Precision.HIGHEST, preferred_element_type=jnp.float32)
        scores = low_back(scores) * ATTN_UNIT_DIM ** (-0.5)
        causal = key_pos[None, :] <= query_pos[:, None]
        scores = jnp.where(causal, scores, -1e+30)
        probs = jax.nn.softmax(scores, axis=-1)
        return jnp.einsum('hgqk,khd->qhgd', low(probs), value_rows, precision=lax.Precision.HIGHEST, preferred_element_type=jnp.float32)
    attended = lax.map(jax.checkpoint(one_block), (block_list, jnp.arange(block_count).astype(jnp.int32)))
    return attended.reshape(series_extent, QUERY_HEADS * ATTN_UNIT_DIM)

def layer(inputs, prenorm_scaling, hidden_gain, query_weight, key_matrix, value_matrix, output_weight, gate_weight, up_weight, down_weight):
    series_extent = inputs.shape[0]
    positions = jnp.arange(series_extent).astype(jnp.int32)
    cosine_table, sine_table = rotary_tables(positions, ATTN_UNIT_DIM)
    inv_one = lax.rsqrt(lax.optimization_barrier(jnp.mean(inputs * inputs, -1, keepdims=True)) + EPS)
    normed_one = low(inputs * inv_one * prenorm_scaling)
    query_projected = low_back(matmul(normed_one, query_weight))
    key_projected = low_back(matmul(normed_one, key_matrix))
    value_projected = low_back(matmul(normed_one, value_matrix))
    query_rows = low(apply_rotation(query_projected.reshape(series_extent, QUERY_HEADS, ATTN_UNIT_DIM), cosine_table, sine_table)).reshape(series_extent, SHARED_KV_UNITS, QUERY_HEADS // SHARED_KV_UNITS, ATTN_UNIT_DIM)
    key_rows = low(apply_rotation(key_projected.reshape(series_extent, SHARED_KV_UNITS, ATTN_UNIT_DIM), cosine_table, sine_table))
    value_rows = low(value_projected).reshape(series_extent, SHARED_KV_UNITS, ATTN_UNIT_DIM)
    attended = low(low_back(attention(query_rows, key_rows, value_rows)))
    hidden_in = inputs + low_back(matmul(attended, output_weight))
    inv_two = lax.rsqrt(lax.optimization_barrier(jnp.mean(hidden_in * hidden_in, -1, keepdims=True)) + EPS)
    normed_two = low(hidden_in * inv_two * hidden_gain)
    gate_val = low_back(matmul(normed_two, gate_weight))
    up_val = low_back(matmul(normed_two, up_weight))
    product = low(jax.nn.silu(gate_val) * up_val)
    return hidden_in + matmul(product, down_weight)

def reference(tokens, cotangent, prenorm_scaling, hidden_gain, query_weight, key_matrix, value_matrix, output_weight, gate_weight, up_weight, down_weight):
    params = tuple((w.astype(jnp.float32) for w in (prenorm_scaling, hidden_gain, query_weight, key_matrix, value_matrix, output_weight, gate_weight, up_weight, down_weight)))

    def one_sequence(totals, pair):
        incoming_series, seq_cot = pair
        result, pullback = jax.vjp(layer, incoming_series.astype(jnp.float32), *params)
        grads = pullback(seq_cot.astype(jnp.float32))
        new_totals = tuple((acc + grad for acc, grad in zip(totals, grads[1:])))
        return (new_totals, (result.astype(jnp.bfloat16), grads[0]))
    zero_filled = tuple((jnp.zeros(p.shape, jnp.float32) for p in params))
    totals, (output, input_grad) = lax.scan(one_sequence, zero_filled, (tokens, cotangent))
    return (output, input_grad, totals[0], totals[1], totals[2], totals[3], totals[4], totals[5], totals[6], totals[7], totals[8])
```

```python
import jax
import jax.numpy as jnp
from jax import lax
from jax.sharding import PartitionSpec as P

QUERY_HEADS = 15
SHARED_KV_UNITS = 5
ATTN_UNIT_DIM = 64
KV_WIDTH = SHARED_KV_UNITS * ATTN_UNIT_DIM
Q_WIDTH = QUERY_HEADS * ATTN_UNIT_DIM

EPS = 1e-05
THETA = 100000.0
F32 = jnp.float32
BF16 = jnp.bfloat16
barrier = lax.optimization_barrier


def rotary_tables(positions, model_width):
    half_width = model_width // 2
    freqs = THETA ** (-(jnp.arange(half_width, dtype=F32) * 2.0 / model_width))
    angles = positions.astype(F32)[:, None] * freqs[None, :]
    return (jnp.cos(angles), jnp.sin(angles))


def apply_rotation(value_rows, cosine_table, sine_table):
    half_width = value_rows.shape[-1] // 2
    former = value_rows[..., :half_width]
    latter = value_rows[..., half_width:]
    cos_rows = cosine_table[:, None, :]
    sin_rows = sine_table[:, None, :]
    return jnp.concatenate(
        [former * cos_rows - latter * sin_rows, latter * cos_rows + former * sin_rows], -1
    )


def inverse_rotation(grads, cosine_table, sine_table):
    return apply_rotation(grads, cosine_table, -sine_table)


def swap_core(block):
    size = lax.axis_size("shard")
    return lax.ppermute(block, "shard", [(i, i ^ 1) for i in range(size)])


def shift_y(block, step):
    size = lax.axis_size("shard")
    return lax.ppermute(block, "shard", [(i, (i + 2 * step) % size) for i in range(size)])


def swap_x(block):
    return lax.ppermute(block, "tensor", [(0, 1), (1, 0)])


def shift_z(block, step):
    size = lax.axis_size("ctx")
    pairs = [(i, i + step) for i in range(size) if 0 <= i + step < size]
    return lax.ppermute(block, "ctx", pairs)


def gather_rows(own, received):
    size = lax.axis_size("shard")
    me = lax.axis_index("shard")
    rows, width = own.shape
    whole = jnp.zeros((size, rows, width), own.dtype)
    for step, block in enumerate([own] + received):
        source = lax.rem(me - 2 * step + size, size)
        other = swap_core(block)
        whole = lax.dynamic_update_slice(whole, block[None], (source, 0, 0))
        whole = lax.dynamic_update_slice(whole, other[None], (jnp.bitwise_xor(source, 1), 0, 0))
    return whole.reshape(size * rows, width)


def from_other_chips(own):
    return [shift_y(own, step) for step in range(1, lax.axis_size("shard") // 2)]


def near_first(columns):
    size = lax.axis_size("shard")
    me = lax.axis_index("shard")
    width = columns.shape[1] // size
    parts = []
    for step in range(size // 2):
        owner = lax.rem(me + 2 * step, size)
        for index in (owner, jnp.bitwise_xor(owner, 1)):
            parts.append(lax.dynamic_slice_in_dim(columns, index * width, width, 1))
    return jnp.concatenate(parts, 1)


def sum_cores(terms):
    size = lax.axis_size("shard")
    split = terms.reshape(size // 2, 2, terms.shape[0] // size, terms.shape[1])
    return split[:, 0].astype(F32) + swap_core(split[:, 1]).astype(F32)


def sum_chips(kept):
    total = kept[0]
    for step in range(1, kept.shape[0]):
        total = total + shift_y(kept[step].astype(BF16), step).astype(F32)
    return total


def sum_ctx(block):
    if lax.axis_size("ctx") != 4:
        return lax.psum(block.astype(BF16), "ctx")
    me = lax.axis_index("ctx")
    inner = jnp.logical_or(me == 1, me == 2)
    edge = lax.ppermute(block.astype(BF16), "ctx", [(0, 1), (3, 2)])
    half = (block.astype(F32) + edge.astype(F32)).astype(BF16)
    swapped = lax.ppermute(half, "ctx", [(1, 2), (2, 1)])
    total = (half.astype(F32) + swapped.astype(F32)).astype(BF16)
    return jnp.where(inner, total, lax.ppermute(total, "ctx", [(1, 0), (2, 3)]))


def halve_x(block):
    half = block.shape[0] // 2
    me = lax.axis_index("tensor")
    kept = lax.dynamic_slice_in_dim(block, me * half, half, 0)
    sent = lax.dynamic_slice_in_dim(block, (1 - me) * half, half, 0)
    return kept + swap_x(sent.astype(BF16)).astype(F32)


def join_x(block):
    other = swap_x(block)
    first = lax.axis_index("tensor") == 0
    return jnp.concatenate(
        [jnp.where(first, block, other), jnp.where(first, other, block)], 0
    ).astype(F32)


def shards(
    tokens,
    cotangent,
    prenorm_scaling,
    hidden_gain,
    query_weight,
    key_matrix,
    value_matrix,
    output_weight,
    gate_weight,
    up_weight,
    down_weight,
):
    group_count = QUERY_HEADS // SHARED_KV_UNITS
    token_rows = tokens.shape[1]
    units = gate_weight.shape[1]
    ctx_size = lax.axis_size("ctx")
    ctx_me = lax.axis_index("ctx")
    tensor_me = lax.axis_index("tensor")
    scale_factor = ATTN_UNIT_DIM ** (-0.5)
    local = jnp.arange(token_rows, dtype=jnp.int32)
    positions = (ctx_me * 2 + tensor_me) * token_rows + local
    cosine_table, sine_table = rotary_tables(positions, ATTN_UNIT_DIM)
    inputs = tokens[0].astype(F32)

    side = jnp.stack([prenorm_scaling, hidden_gain], 1).astype(BF16)
    own_kv = jnp.concatenate([key_matrix, value_matrix, jnp.pad(side, ((0, 0), (0, 62)))], 1)
    own_ffn = jnp.concatenate([gate_weight, up_weight, output_weight], 1)
    own_down = down_weight.T
    far_kv = from_other_chips(own_kv)
    other_cotangent = swap_x(cotangent[0])
    far_kv, query_weight = barrier((far_kv, query_weight))
    far_query = from_other_chips(query_weight)
    first = gather_rows(own_kv, far_kv)
    gains = first[:, 2 * KV_WIDTH :].astype(F32).T
    gain_one, gain_two = gains[0], gains[1]

    inv_one = lax.rsqrt(jnp.mean(inputs * inputs, -1, keepdims=True) + EPS)
    normed_one = (inputs * inv_one * gain_one).astype(BF16)
    projected = jnp.dot(normed_one, first[:, : 2 * KV_WIDTH], preferred_element_type=F32)
    key_rows = (
        apply_rotation(
            projected[:, :KV_WIDTH].reshape(token_rows, SHARED_KV_UNITS, ATTN_UNIT_DIM),
            cosine_table,
            sine_table,
        )
        .astype(BF16)
        .reshape(token_rows, KV_WIDTH)
    )
    value_rows = projected[:, KV_WIDTH:].astype(BF16)
    key_value = jnp.concatenate([key_rows, value_rows], 1)
    far_query, own_ffn, key_value = barrier((far_query, own_ffn, key_value))
    far_ffn = from_other_chips(own_ffn)
    full_query = gather_rows(query_weight, far_query)
    query_projected = jnp.dot(normed_one, full_query, preferred_element_type=F32)
    grouped_heads = (
        apply_rotation(
            query_projected.reshape(token_rows, QUERY_HEADS, ATTN_UNIT_DIM),
            cosine_table,
            sine_table,
        )
        .astype(BF16)
        .reshape(token_rows, SHARED_KV_UNITS, group_count, ATTN_UNIT_DIM)
    )

    def valid_keys(step):
        start = (ctx_me - step) * 2
        key_pos = jnp.concatenate(
            [(start + tensor_me) * token_rows + local, (start + 1 - tensor_me) * token_rows + local]
        )
        return (key_pos[None, :] <= positions[:, None]) & (key_pos[None, :] >= 0)

    def forward_block(state, both, step):
        peak_score, totals, accum = state
        both = both.reshape(2 * token_rows, 2, SHARED_KV_UNITS, ATTN_UNIT_DIM)
        valid = valid_keys(step)
        scores = (
            jnp.einsum("qhgd,khd->hgqk", grouped_heads, both[:, 0], preferred_element_type=F32)
            * scale_factor
        )
        scores = jnp.where(valid, scores, -1e30)
        new_peak = jnp.maximum(peak_score, jnp.max(scores, -1))
        rescale = jnp.exp(peak_score - new_peak)
        probs = jnp.where(valid, jnp.exp(scores - new_peak[..., None]), 0.0)
        totals = totals * rescale + jnp.sum(probs, -1)
        accum = accum * rescale[..., None] + jnp.einsum(
            "hgqk,khd->hgqd", probs.astype(BF16), both[:, 1], preferred_element_type=F32
        )
        return (new_peak, totals, accum)

    state = (
        jnp.full((SHARED_KV_UNITS, group_count, token_rows), -1e30, F32),
        jnp.zeros((SHARED_KV_UNITS, group_count, token_rows), F32),
        jnp.zeros((SHARED_KV_UNITS, group_count, token_rows, ATTN_UNIT_DIM), F32),
    )
    unrolled = ctx_size <= 4
    blocks = []
    passing = key_value
    for step in range(ctx_size):
        if step > 0:
            passing = shift_z(passing, 1)
        both = jnp.concatenate([passing, swap_x(passing)], 0)
        blocks.append(both)
        if unrolled:
            state = forward_block(state, both, step)
    if not unrolled:
        stacked = jnp.stack(blocks)
        steps = jnp.arange(ctx_size, dtype=jnp.int32)
        state, unused = lax.scan(
            lambda held, item: (forward_block(held, item[0], item[1]), None),
            state,
            (stacked, steps),
        )
    peak_score, totals, accum = state
    attended = accum / totals[..., None]
    log_total = peak_score + jnp.log(totals)
    far_ffn, own_down, attended = barrier((far_ffn, own_down, attended))
    far_down = from_other_chips(own_down)
    attended_low = attended.transpose(2, 0, 1, 3).reshape(token_rows, Q_WIDTH).astype(BF16)

    second = gather_rows(own_ffn, far_ffn)
    full_output = second[:, 2 * units :]
    gate_up = second[:, : 2 * units]
    branch = jnp.dot(attended_low, full_output, preferred_element_type=F32)
    hidden_in = inputs + branch
    inv_two = lax.rsqrt(jnp.mean(hidden_in * hidden_in, -1, keepdims=True) + EPS)
    normed_two = (hidden_in * inv_two * gain_two).astype(BF16)
    other_normed = swap_x(normed_two)
    normed_all = jnp.concatenate([normed_two, other_normed], 0)
    upstream_all = jnp.concatenate([cotangent[0], other_cotangent], 0)
    upstream = cotangent[0].astype(F32)
    down_full = gather_rows(own_down, far_down)
    d_product = jnp.dot(upstream_all, down_full, preferred_element_type=F32)
    inner = jnp.dot(normed_all, gate_up, preferred_element_type=F32)
    gate_val = inner[:, :units]
    up_val = inner[:, units:]
    sigmoid_gate = jax.nn.sigmoid(gate_val)
    product_low = (gate_val * sigmoid_gate * up_val).astype(BF16)
    d_up = (d_product * gate_val * sigmoid_gate).astype(BF16)
    d_gate = (d_product * up_val * sigmoid_gate * (1.0 + gate_val * (1.0 - sigmoid_gate))).astype(
        BF16
    )
    d_inner = jnp.concatenate([d_gate, d_up], 1)
    d_normed_sent = jnp.einsum(
        "tf,df->td", d_inner[token_rows:], gate_up, preferred_element_type=F32
    ).astype(BF16)
    d_normed_came = swap_x(d_normed_sent)
    near_normed = near_first(normed_all)
    grad_inner = jnp.einsum(
        "td,tf->df", near_normed, d_inner, preferred_element_type=F32
    ).astype(BF16)
    grad_down = jnp.einsum(
        "td,tf->df", near_first(upstream_all), product_low, preferred_element_type=F32
    ).astype(BF16)
    d_normed_own = jnp.einsum(
        "tf,df->td", d_inner[:token_rows], gate_up, preferred_element_type=F32
    )
    d_normed_came, grad_inner, grad_down, d_normed_own = barrier(
        (d_normed_came, grad_inner, grad_down, d_normed_own)
    )
    d_normed_two = d_normed_own + d_normed_came.astype(F32)
    feed_parts = jnp.einsum("tf,df->td", product_low, down_full, preferred_element_type=F32)
    feed = feed_parts[:token_rows] + swap_x(feed_parts[token_rows:].astype(BF16)).astype(F32)
    result = (hidden_in + feed).astype(BF16)[None]

    grad_gain_two = jnp.sum(d_normed_two * hidden_in * inv_two, 0)
    scaled_two = d_normed_two * gain_two
    d_hidden = (
        upstream
        + inv_two * scaled_two
        - hidden_in * inv_two**3 * jnp.mean(scaled_two * hidden_in, -1, keepdims=True)
    )
    d_branch = d_hidden.astype(BF16)
    attended_grad = jnp.einsum("td,ed->te", d_branch, full_output, preferred_element_type=F32)
    grad_output = jnp.einsum(
        "te,td->ed", near_first(attended_low), d_branch, preferred_element_type=F32
    ).astype(BF16)
    attended_low_grad = attended_grad.astype(BF16)
    attended_low_grad, grad_output, grad_inner, grad_down = barrier(
        (attended_low_grad, grad_output, grad_inner, grad_down)
    )
    attended_low_grad = attended_low_grad.reshape(
        token_rows, SHARED_KV_UNITS, group_count, ATTN_UNIT_DIM
    )

    down_total = sum_chips(sum_cores(grad_down))
    inner_total = sum_chips(sum_cores(grad_inner))
    output_total = sum_chips(sum_cores(grad_output))
    out_down = sum_ctx(down_total).T.astype(F32)
    out_gate = sum_ctx(inner_total[:, :units]).astype(F32)
    out_up = sum_ctx(inner_total[:, units:]).astype(F32)
    out_output = join_x(sum_ctx(halve_x(output_total)))

    delta = jnp.einsum(
        "qhgd,hgqd->hgq", attended_low_grad.astype(F32), attended, preferred_element_type=F32
    )

    def backward_block(asker_cotangent, both, step):
        both = both.reshape(2 * token_rows, 2, SHARED_KV_UNITS, ATTN_UNIT_DIM)
        valid = valid_keys(step)
        scores = (
            jnp.einsum("qhgd,khd->hgqk", grouped_heads, both[:, 0], preferred_element_type=F32)
            * scale_factor
        )
        probs = jnp.where(valid, jnp.exp(scores - log_total[..., None]), 0.0)
        d_probs = jnp.einsum(
            "qhgd,khd->hgqk", attended_low_grad, both[:, 1], preferred_element_type=F32
        )
        d_scores = (scale_factor * probs * (d_probs - delta[..., None])).astype(BF16)
        value_gradient = jnp.einsum(
            "hgqk,qhgd->khd", probs.astype(BF16), attended_low_grad, preferred_element_type=F32
        )
        key_gradient = jnp.einsum(
            "hgqk,qhgd->khd", d_scores, grouped_heads, preferred_element_type=F32
        )
        asker_cotangent = asker_cotangent + jnp.einsum(
            "hgqk,khd->qhgd", d_scores, both[:, 0], preferred_element_type=F32
        )
        joined = jnp.concatenate(
            [
                key_gradient.reshape(2 * token_rows, KV_WIDTH),
                value_gradient.reshape(2 * token_rows, KV_WIDTH),
            ],
            1,
        )
        return asker_cotangent, joined

    asker_cotangent = jnp.zeros((token_rows, SHARED_KV_UNITS, group_count, ATTN_UNIT_DIM), F32)
    if not unrolled:
        asker_cotangent, terms = lax.scan(
            lambda held, item: backward_block(held, item[0], item[1]),
            asker_cotangent,
            (stacked, steps),
        )
    arriving = None
    for step in reversed(range(ctx_size)):
        if unrolled:
            asker_cotangent, joined = backward_block(asker_cotangent, blocks[step], step)
        else:
            joined = terms[step]
        part = joined[:token_rows] + swap_x(joined[token_rows:].astype(BF16)).astype(F32)
        if arriving is not None:
            part = part + arriving.astype(F32)
        if step > 0:
            arriving = shift_z(part.astype(BF16), -1)
    key_value_grad = part
    d_query_low = (
        inverse_rotation(
            asker_cotangent.reshape(token_rows, QUERY_HEADS, ATTN_UNIT_DIM),
            cosine_table,
            sine_table,
        )
        .reshape(token_rows, Q_WIDTH)
        .astype(BF16)
    )
    near_one = near_first(normed_one)
    grad_query = jnp.einsum(
        "td,te->de", near_one, d_query_low, preferred_element_type=F32
    ).astype(BF16)
    query_total = sum_chips(sum_cores(grad_query))
    out_query = join_x(sum_ctx(halve_x(query_total)))
    d_normed_query = jnp.einsum("te,de->td", d_query_low, full_query, preferred_element_type=F32)
    d_key_low = (
        inverse_rotation(
            key_value_grad[:, :KV_WIDTH].reshape(token_rows, SHARED_KV_UNITS, ATTN_UNIT_DIM),
            cosine_table,
            sine_table,
        )
        .reshape(token_rows, KV_WIDTH)
        .astype(BF16)
    )
    value_low_grad = key_value_grad[:, KV_WIDTH:].astype(BF16)
    d_projected = jnp.concatenate([d_key_low, value_low_grad], 1)
    grad_kv = jnp.einsum(
        "td,te->de", near_one, d_projected, preferred_element_type=F32
    ).astype(BF16)
    d_normed_one = d_normed_query + jnp.einsum(
        "te,de->td", d_projected, first[:, : 2 * KV_WIDTH], preferred_element_type=F32
    )
    grad_gain_one = jnp.sum(d_normed_one * inputs * inv_one, 0)
    scaled_one = d_normed_one * gain_one
    d_inputs = (
        d_hidden
        + inv_one * scaled_one
        - inputs * inv_one**3 * jnp.mean(scaled_one * inputs, -1, keepdims=True)
    )
    gain_grads = near_first(jnp.stack([grad_gain_one, grad_gain_two], 0)).T.astype(BF16)
    last = jnp.concatenate([grad_kv, jnp.pad(gain_grads, ((0, 0), (0, 62)))], 1)
    last = join_x(sum_ctx(halve_x(sum_chips(sum_cores(last)))))
    return (
        result,
        d_inputs[None],
        last[:, 2 * KV_WIDTH],
        last[:, 2 * KV_WIDTH + 1],
        out_query,
        last[:, :KV_WIDTH],
        last[:, KV_WIDTH : 2 * KV_WIDTH],
        out_output,
        out_gate,
        out_up,
        out_down,
    )


def solution(mesh):
    return jax.shard_map(
        shards,
        mesh=mesh,
        in_specs=(
            P("shard", ("ctx", "tensor"), None),
            P("shard", ("ctx", "tensor"), None),
            P("shard"),
            P("shard"),
            P("shard", None),
            P("shard", None),
            P("shard", None),
            P("shard", None),
            P("shard", "tensor"),
            P("shard", "tensor"),
            P("tensor", "shard"),
        ),
        out_specs=(
            P("shard", ("ctx", "tensor"), None),
            P("shard", ("ctx", "tensor"), None),
            P("shard"),
            P("shard"),
            P("shard", None),
            P("shard", None),
            P("shard", None),
            P("shard", None),
            P("shard", "tensor"),
            P("shard", "tensor"),
            P("tensor", "shard"),
        ),
        check_vma=False,
    )
```

```python
import functools

import jax
import jax.numpy as jnp
from jax import lax
from jax.experimental import pallas as pl
from jax.experimental.pallas import tpu as pltpu
from jax.sharding import PartitionSpec as P

QUERY_HEADS = 15
SHARED_KV_UNITS = 5
ATTN_UNIT_DIM = 64
GROUP = QUERY_HEADS // SHARED_KV_UNITS
KV_WIDTH = SHARED_KV_UNITS * ATTN_UNIT_DIM
Q_WIDTH = QUERY_HEADS * ATTN_UNIT_DIM

EPS = 1e-05
THETA = 100000.0
F32 = jnp.float32
BF16 = jnp.bfloat16
barrier = lax.optimization_barrier


def rotary_tables(positions):
    half = ATTN_UNIT_DIM // 2
    freqs = THETA ** (-(jnp.arange(half, dtype=F32) * 2.0 / ATTN_UNIT_DIM))
    angles = freqs[:, None] * positions.astype(F32)[None, :]
    return (jnp.cos(angles), jnp.sin(angles))


def rotate(block, cosine, sine):
    split = block.reshape(-1, 2, ATTN_UNIT_DIM // 2, block.shape[1])
    former, latter = split[:, 0], split[:, 1]
    turned = jnp.stack([former * cosine - latter * sine, latter * cosine + former * sine], 1)
    return turned.reshape(block.shape)


def rotate_lanes(block, cosine, sine):
    split = block.reshape(block.shape[0], -1, 2, ATTN_UNIT_DIM // 2)
    former, latter = split[:, :, 0], split[:, :, 1]
    cosine, sine = cosine[:, None, :], sine[:, None, :]
    turned = jnp.stack([former * cosine - latter * sine, latter * cosine + former * sine], 2)
    return turned.reshape(block.shape)


def product(left, right, left_dim, right_dim):
    return lax.dot_general(
        left, right, (((left_dim,), (right_dim,)), ((), ())), preferred_element_type=F32
    )


def swap_core(block):
    size = lax.axis_size("shard")
    return lax.ppermute(block, "shard", [(i, i ^ 1) for i in range(size)])


def shift_y(block, step):
    size = lax.axis_size("shard")
    return lax.ppermute(block, "shard", [(i, (i + 2 * step) % size) for i in range(size)])


def swap_x(block):
    return lax.ppermute(block, "tensor", [(0, 1), (1, 0)])


def shift_z(block, step):
    size = lax.axis_size("ctx")
    pairs = [(i, i + step) for i in range(size) if 0 <= i + step < size]
    return lax.ppermute(block, "ctx", pairs)


def from_other_chips(own):
    return [shift_y(own, -step) for step in range(1, lax.axis_size("shard") // 2)]


def both_cores(held):
    return [piece for block in held for piece in (block, swap_core(block))]


def near_places():
    size = lax.axis_size("shard")
    me = lax.axis_index("shard")
    places = []
    for step in range(size // 2):
        owner = lax.rem(me + 2 * step, size)
        places += [owner, jnp.bitwise_xor(owner, 1)]
    return places


def near_pieces(whole, dim):
    width = whole.shape[dim] // lax.axis_size("shard")
    return [lax.dynamic_slice_in_dim(whole, p * width, width, dim) for p in near_places()]


def in_order(pieces, dim):
    places = near_places()
    ordered = []
    for index in range(len(pieces)):
        piece = pieces[0]
        for place, other in zip(places[1:], pieces[1:]):
            piece = jnp.where(place == index, other, piece)
        ordered.append(piece)
    return jnp.concatenate(ordered, dim)


def add_low(left, right):
    return (left.astype(F32) + right.astype(F32)).astype(BF16)


def block_sums(kept, came):
    return [add_low(kept[step], came[step]) for step in range(kept.shape[0])]


def chip_sends(kept):
    return [shift_y(block, step) for step, block in enumerate(kept) if step > 0]


def chip_sum(kept, came):
    total = kept[0].astype(F32)
    for block in came:
        total = total + block.astype(F32)
    return total.astype(BF16)


def on_line():
    return lax.axis_size("ctx") == 4


def line_in(block):
    return lax.ppermute(block, "ctx", [(0, 1), (3, 2)]) if on_line() else block


def line_mid(half):
    return lax.ppermute(half, "ctx", [(1, 2), (2, 1)]) if on_line() else half


def line_out(total):
    return lax.ppermute(total, "ctx", [(1, 0), (2, 3)]) if on_line() else total


def line_half(block, came):
    return add_low(block, came) if on_line() else lax.psum(block, "ctx")


def line_total(half, came):
    return add_low(half, came) if on_line() else half


def line_result(total, came):
    if not on_line():
        return total
    me = lax.axis_index("ctx")
    return jnp.where(jnp.logical_or(me == 1, me == 2), total, came)


def x_parts(block):
    half = block.shape[0] // 2
    me = lax.axis_index("tensor")
    kept = lax.dynamic_slice_in_dim(block, me * half, half, 0)
    sent = lax.dynamic_slice_in_dim(block, (1 - me) * half, half, 0)
    return kept, sent


def x_join(block, other):
    first = lax.axis_index("tensor") == 0
    return jnp.concatenate(
        [jnp.where(first, block, other), jnp.where(first, other, block)], 0
    ).astype(F32)


def head_part(head, offset=0):
    return slice(offset + head * ATTN_UNIT_DIM, offset + (head + 1) * ATTN_UNIT_DIM)


def causal_mask(keys, lanes, rows):
    key = lax.broadcasted_iota(jnp.int32, (keys, lanes), 0)
    lane = lax.broadcasted_iota(jnp.int32, (keys, lanes), 1)
    return key <= lax.rem(lane, rows)


def forward_first_kernel(query_ref, tile_ref, stats_ref, accum_ref):
    rows = tile_ref.shape[0]
    lanes = query_ref.shape[1]
    mask = causal_mask(rows, lanes, rows)
    stats_ref[...] = jnp.zeros_like(stats_ref)
    for head in range(SHARED_KV_UNITS):
        key = tile_ref[:, head_part(head)]
        value = tile_ref[:, head_part(head, KV_WIDTH)]
        scores = jnp.dot(key, query_ref[head_part(head), :], preferred_element_type=F32)
        scores = jnp.where(mask, scores, -1e30)
        peak = jnp.max(scores, 0, keepdims=True)
        probs = jnp.exp(scores - peak)
        stats_ref[head : head + 1, :] = peak
        stats_ref[8 + head : 9 + head, :] = jnp.sum(probs, 0, keepdims=True)
        accum_ref[head_part(head), :] = product(value, probs.astype(BF16), 0, 0)


def forward_kernel(count, flags_ref, query_ref, *refs):
    tiles, (stats_in, accum_in, stats_ref, accum_ref) = refs[:count], refs[count:]
    stats_ref[...] = stats_in[...]
    accum_ref[...] = accum_in[...]
    for index, tile_ref in enumerate(tiles):

        @pl.when(flags_ref[index] != 0)
        def _(tile_ref=tile_ref):
            for head in range(SHARED_KV_UNITS):
                key = tile_ref[:, head_part(head)]
                value = tile_ref[:, head_part(head, KV_WIDTH)]
                scores = jnp.dot(key, query_ref[head_part(head), :], preferred_element_type=F32)
                old_peak = stats_ref[head : head + 1, :]
                peak = jnp.maximum(old_peak, jnp.max(scores, 0, keepdims=True))
                probs = jnp.exp(scores - peak)
                rescale = jnp.exp(old_peak - peak)
                total = stats_ref[8 + head : 9 + head, :]
                stats_ref[head : head + 1, :] = peak
                stats_ref[8 + head : 9 + head, :] = total * rescale + jnp.sum(
                    probs, 0, keepdims=True
                )
                accum_ref[head_part(head), :] = accum_ref[head_part(head), :] * rescale + (
                    product(value, probs.astype(BF16), 0, 0)
                )


def backward_kernel(causal, count, flags_ref, query_ref, grad_ref, stats_ref, *refs):
    tiles, (into, out_ref), sums = refs[:count], refs[count : count + 2], refs[count + 2 :]
    rows = tiles[0].shape[0]
    lanes = query_ref.shape[1]
    out_ref[...] = into[...]
    for index, (tile_ref, sum_ref) in enumerate(zip(tiles, sums)):

        @pl.when(flags_ref[index] == 0)
        def _(sum_ref=sum_ref):
            sum_ref[...] = jnp.zeros_like(sum_ref)

        @pl.when(flags_ref[index] != 0)
        def _(tile_ref=tile_ref, sum_ref=sum_ref):
            for head in range(SHARED_KV_UNITS):
                key = tile_ref[:, head_part(head)]
                value = tile_ref[:, head_part(head, KV_WIDTH)]
                query = query_ref[head_part(head), :]
                grad = grad_ref[head_part(head), :]
                scores = jnp.dot(key, query, preferred_element_type=F32)
                probs = jnp.exp(scores - stats_ref[head : head + 1, :])
                if causal:
                    probs = jnp.where(causal_mask(rows, lanes, rows), probs, 0.0)
                d_probs = jnp.dot(value, grad, preferred_element_type=F32)
                d_scores = (probs * (d_probs - stats_ref[8 + head : 9 + head, :])).astype(BF16)
                sum_ref[:, head_part(head)] = product(d_scores, query, 1, 1).astype(BF16)
                sum_ref[:, head_part(head, KV_WIDTH)] = product(
                    probs.astype(BF16), grad, 1, 1
                ).astype(BF16)
                out_ref[head_part(head), :] += product(key, d_scores, 0, 0)


def cost(multiply_adds, values=0, transcendentals=0):
    return pl.CostEstimate(
        flops=2 * multiply_adds, bytes_accessed=values, transcendentals=transcendentals
    )


def tile_cost(count, rows, lanes, matmuls):
    return cost(
        4 * matmuls * count * rows * lanes * KV_WIDTH,
        8 * KV_WIDTH * lanes,
        count * rows * lanes * SHARED_KV_UNITS,
    )


MEMORY = pltpu.CompilerParams(vmem_limit_bytes=24 * 1024 * 1024)
LARGE = pltpu.CompilerParams(vmem_limit_bytes=58 * 1024 * 1024)
IN_VMEM = pl.BlockSpec(memory_space=pltpu.VMEM)
IN_SMEM = pl.BlockSpec(memory_space=pltpu.SMEM)


def on_core(
    kernel, name, out_shape, *operands, estimate, scratch=(), first_in_smem=True, columns=None
):
    def block(shape):
        return pl.BlockSpec(shape, lambda i: (0,) * len(shape))

    specs = [IN_VMEM] * len(operands)
    outs = [IN_VMEM] * len(out_shape)
    if columns is not None:
        last = operands[-1].shape
        specs = [
            block((last[0], columns) if operand.shape == last else operand.shape)
            for operand in operands
        ]
        outs = [block(shape[0]) for shape in out_shape]
    if first_in_smem:
        specs[0] = IN_SMEM
    return pl.pallas_call(
        kernel,
        grid=() if columns is None else (1,),
        in_specs=specs,
        out_specs=tuple(outs),
        out_shape=tuple(jax.ShapeDtypeStruct(*shape) for shape in out_shape),
        scratch_shapes=list(scratch),
        cost_estimate=estimate,
        compiler_params=MEMORY if columns is None else LARGE,
        name=name,
    )(*operands)


def forward_first(query, tile):
    lanes = query.shape[1]
    return on_core(
        forward_first_kernel,
        "attend_own",
        (((16, lanes), F32), ((KV_WIDTH, lanes), F32)),
        query,
        tile,
        estimate=tile_cost(1, tile.shape[0], lanes, 2),
        first_in_smem=False,
    )


def forward_tiles(query, tiles, flags, stats, accum):
    return on_core(
        functools.partial(forward_kernel, len(tiles)),
        "attend",
        ((stats.shape, F32), (accum.shape, F32)),
        jnp.stack(flags).astype(jnp.int32),
        query,
        *tiles,
        stats,
        accum,
        estimate=tile_cost(len(tiles), tiles[0].shape[0], query.shape[1], 2),
    )


def backward_tiles(query, grad, stats, tiles, flags, into, causal=False):
    out = on_core(
        functools.partial(backward_kernel, causal, len(tiles)),
        "attend_back",
        ((into.shape, F32),) + ((tiles[0].shape, BF16),) * len(tiles),
        jnp.stack(flags).astype(jnp.int32),
        query,
        grad,
        stats,
        *tiles,
        into,
        estimate=tile_cost(len(tiles), tiles[0].shape[0], query.shape[1], 5),
    )
    return out[0], out[1:]


def to_lanes(block):
    rows = block.shape[1]
    split = block.reshape(SHARED_KV_UNITS, GROUP, ATTN_UNIT_DIM, rows)
    return split.transpose(0, 2, 1, 3).reshape(KV_WIDTH, GROUP * rows)


def place_rows(places, index, width):
    return pl.ds(pl.multiple_of(places[index] * width, 16), width)


def put_in_order(places, pieces, whole, columns):
    width = pieces[0].shape[0]
    for index, piece in enumerate(pieces):
        whole[place_rows(places, index, width), :] = piece[:, :columns]


def mid_kernel(count, places, stats, accum, inputs, gain, *refs):
    weights = refs[:count]
    attended_ref, hidden_ref, normed_ref, weight = refs[count:]
    rows, model = inputs.shape
    put_in_order(places, weights, weight, model)
    for head in range(SHARED_KV_UNITS):
        part = accum[head_part(head), :] / stats[8 + head : 9 + head, :]
        for member in range(GROUP):
            attended_ref[head_part(head * GROUP + member), :] = part[
                :, member * rows : (member + 1) * rows
            ].astype(BF16)
    hidden = inputs[...].astype(F32) + product(attended_ref[...], weight[...], 0, 0)
    hidden_ref[...] = hidden
    inverse = lax.rsqrt(jnp.mean(hidden * hidden, -1, keepdims=True) + EPS)
    normed_ref[...] = (hidden * inverse * gain[...]).astype(BF16)


def feed_kernel(count, places, *refs):
    normed_own, normed_other, upstream_own, upstream_other = refs[:4]
    gates, ups, downs = (refs[4 + k * count : 4 + (k + 1) * count] for k in range(3))
    units_ref, feed_own, feed_other, grad_own, grad_other = refs[4 + 3 * count : 9 + 3 * count]
    gate, up, down, normed, upstream, feed_sum, grad_sum = refs[9 + 3 * count :]
    rows = normed_own.shape[0]
    tile = gate.shape[1]

    @pl.when(pl.program_id(0) == 0)
    def _():
        normed[:rows, :] = normed_own[...]
        normed[rows:, :] = normed_other[...]
        upstream[:rows, :] = upstream_own[...]
        upstream[rows:, :] = upstream_other[...]
        feed_sum[...] = jnp.zeros_like(feed_sum)
        grad_sum[...] = jnp.zeros_like(grad_sum)

    for pieces, whole in ((gates, gate), (ups, up), (downs, down)):
        put_in_order(places, pieces, whole, tile)
    gate_val = jnp.dot(normed[...], gate[...], preferred_element_type=F32)
    up_val = jnp.dot(normed[...], up[...], preferred_element_type=F32)
    d_product = jnp.dot(upstream[...], down[...], preferred_element_type=F32)
    sigmoid = 1.0 / (1.0 + jnp.exp(-gate_val))
    silu = gate_val * sigmoid
    z = (silu * up_val).astype(BF16)
    d_up = (d_product * silu).astype(BF16)
    d_gate = (d_product * up_val * sigmoid * (1.0 + gate_val * (1.0 - sigmoid))).astype(BF16)
    units_ref[:, :tile] = z
    units_ref[:, tile : 2 * tile] = d_gate
    units_ref[:, 2 * tile :] = d_up
    grad_sum[...] += product(d_gate, gate[...], 1, 1) + product(d_up, up[...], 1, 1)
    feed_sum[...] += product(z, down[...], 1, 1)

    @pl.when(pl.program_id(0) == pl.num_programs(0) - 1)
    def _():
        for total, own, other in ((feed_sum, feed_own, feed_other), (grad_sum, grad_own, grad_other)):
            own[...] = total[:rows, :]
            other[...] = total[rows:, :].astype(BF16)


def feed_tile(units):
    return 256 if units % 256 == 0 else 128


def feed_forward(places, rows_in, packed, units):
    count = len(packed)
    rows, model = rows_in[0].shape
    width = packed[0].shape[0]
    tile = feed_tile(units)
    steps = units // tile
    whole = pl.BlockSpec((rows, model), lambda i: (0, 0))
    gate_spec = pl.BlockSpec((width, tile), lambda i: (0, i))
    up_spec = pl.BlockSpec((width, tile), lambda i: (0, i + steps))
    down_spec = pl.BlockSpec((width, tile), lambda i: (0, i + 2 * steps))
    out_spec = pl.BlockSpec((2 * rows, 3 * tile), lambda i: (0, i))
    return pl.pallas_call(
        functools.partial(feed_kernel, count),
        grid=(steps,),
        in_specs=[IN_SMEM]
        + [whole] * 4
        + [gate_spec] * count
        + [up_spec] * count
        + [down_spec] * count,
        out_specs=(out_spec,) + (whole,) * 4,
        out_shape=(jax.ShapeDtypeStruct((2 * rows, 3 * units), BF16),)
        + (
            jax.ShapeDtypeStruct((rows, model), F32),
            jax.ShapeDtypeStruct((rows, model), BF16),
        )
        * 2,
        scratch_shapes=[pltpu.VMEM((model, tile), BF16)] * 3
        + [pltpu.VMEM((2 * rows, model), BF16)] * 2
        + [pltpu.VMEM((2 * rows, model), F32)] * 2,
        cost_estimate=cost(12 * rows * model * units, 6 * model * units, rows * units),
        compiler_params=LARGE,
        name="feed_forward",
    )(places, *rows_in, *packed, *packed, *packed)


def grad_kernel(count, width, places, *refs):
    normed_own, normed_other, upstream_own, upstream_other, values, kept, sent = refs
    rows = normed_own.shape[1]

    def sums(own, other):
        for index in range(count):
            part = place_rows(places, index, width)
            total = jnp.dot(
                own[part, :], values[:rows, :], preferred_element_type=F32
            ) + jnp.dot(other[part, :], values[rows:, :], preferred_element_type=F32)
            (kept, sent)[index % 2][index // 2] = total.astype(BF16)

    @pl.when(lax.rem(pl.program_id(0), 3) == 0)
    def _():
        sums(upstream_own, upstream_other)

    @pl.when(lax.rem(pl.program_id(0), 3) != 0)
    def _():
        sums(normed_own, normed_other)


def feed_grads(places, turned, values, units):
    count = lax.axis_size("shard")
    model, rows = turned[0].shape
    width = model // count
    tile = feed_tile(units)
    steps = units // tile
    whole = pl.BlockSpec((model, rows), lambda i: (0, 0))
    sum_spec = pl.BlockSpec((count // 2, width, tile), lambda i: (0, 0, i % 3 * steps + i // 3))
    return pl.pallas_call(
        functools.partial(grad_kernel, count, width),
        grid=(3 * steps,),
        in_specs=[IN_SMEM]
        + [whole] * 4
        + [pl.BlockSpec((2 * rows, tile), lambda i: (0, i))],
        out_specs=(sum_spec,) * 2,
        out_shape=(jax.ShapeDtypeStruct((count // 2, width, 3 * units), BF16),) * 2,
        cost_estimate=cost(6 * rows * model * units, 12 * model * units),
        compiler_params=LARGE,
        name="feed_grads",
    )(places, *turned, values)


def turn_kernel(count, places, *refs):
    own, came, hidden_ref, upstream, gain, attended, accum, stats = refs[:8]
    weights = refs[8 : 8 + count]
    d_hidden_ref, grads, stats_ref, kept, sent, gain_ref, turned = refs[8 + count :]
    rows, model = hidden_ref.shape
    width = weights[0].shape[0]
    hidden = hidden_ref[...]
    d_normed = own[...] + came[...].astype(F32)
    inverse = lax.rsqrt(jnp.mean(hidden * hidden, -1, keepdims=True) + EPS)
    gain_ref[...] = jnp.sum(d_normed * hidden * inverse, 0, keepdims=True)
    scaled = d_normed * gain[...]
    d_hidden = (
        upstream[...].astype(F32)
        + inverse * scaled
        - hidden * (inverse * inverse * inverse * jnp.mean(scaled * hidden, -1, keepdims=True))
    )
    d_hidden_ref[...] = d_hidden
    d_branch = d_hidden.astype(BF16)
    for index, weight in enumerate(weights):
        part = place_rows(places, index, width)
        turned[part, :] = product(weight[:, :model], d_branch, 1, 1).astype(BF16)
        (kept, sent)[index % 2][index // 2] = jnp.dot(
            attended[part, :], d_branch, preferred_element_type=F32
        ).astype(BF16)
    stats_ref[...] = jnp.zeros_like(stats_ref)
    for head in range(SHARED_KV_UNITS):
        for member in range(GROUP):
            lanes = slice(member * rows, (member + 1) * rows)
            grads[head_part(head), lanes] = turned[head_part(head * GROUP + member), :]
        total = stats[8 + head : 9 + head, :]
        stats_ref[head : head + 1, :] = stats[head : head + 1, :] + jnp.log(total)
        stats_ref[8 + head : 9 + head, :] = jnp.sum(
            grads[head_part(head), :].astype(F32) * (accum[head_part(head), :] / total),
            0,
            keepdims=True,
        )


def query_kernel(count, places, d_query, cosine, sine, normed, *refs):
    weights = refs[:count]
    kept, sent, d_rows, turned = refs[count:]
    rows = normed.shape[1]
    width = weights[0].shape[0]
    half = ATTN_UNIT_DIM // 2
    scale = ATTN_UNIT_DIM ** (-0.5)
    for head in range(SHARED_KV_UNITS):
        for member in range(GROUP):
            lanes = slice(member * rows, (member + 1) * rows)
            start = head * ATTN_UNIT_DIM
            former = d_query[start : start + half, lanes] * scale
            latter = d_query[start + half : start + 2 * half, lanes] * scale
            start = (head * GROUP + member) * ATTN_UNIT_DIM
            turned[start : start + half, :] = (
                former * cosine[...] + latter * sine[...]
            ).astype(BF16)
            turned[start + half : start + 2 * half, :] = (
                latter * cosine[...] - former * sine[...]
            ).astype(BF16)
    for index, weight in enumerate(weights):
        part = place_rows(places, index, width)
        (kept, sent)[index % 2][index // 2] = product(normed[part, :], turned[...], 1, 1).astype(
            BF16
        )
        d_rows[part, :] = jnp.dot(weight[...], turned[...], preferred_element_type=F32)


def key_kernel(count, places, *refs):
    own, pair, passing, cosine, sine, normed, inputs, inverse, d_query_rows, gain = refs[:10]
    weights = refs[10 : 10 + count]
    kept, sent, d_rows, turned = refs[10 + count :]
    width = weights[0].shape[0]
    half = ATTN_UNIT_DIM // 2
    total = own[...].astype(F32) + pair[...].astype(F32) + passing[...].astype(F32)
    for head in range(SHARED_KV_UNITS):
        start = head * ATTN_UNIT_DIM
        former = total[:, start : start + half]
        latter = total[:, start + half : start + 2 * half]
        turned[:, start : start + half] = (former * cosine[...] + latter * sine[...]).astype(BF16)
        turned[:, start + half : start + 2 * half] = (
            latter * cosine[...] - former * sine[...]
        ).astype(BF16)
    turned[:, KV_WIDTH:] = total[:, KV_WIDTH:].astype(BF16)
    for index, weight in enumerate(weights):
        part = place_rows(places, index, width)
        d_part = d_query_rows[part, :] + product(weight[:, : 2 * KV_WIDTH], turned[...], 1, 1)
        d_rows[part, :] = d_part
        own_gain = jnp.sum(
            d_part * inputs[part, :].astype(F32) * inverse[...], 1, keepdims=True
        )
        target = (kept, sent)[index % 2]
        target[index // 2, :, : 2 * KV_WIDTH] = jnp.dot(
            normed[part, :], turned[...], preferred_element_type=F32
        ).astype(BF16)
        side = target.shape[2] - 2 * KV_WIDTH
        lane = lax.broadcasted_iota(jnp.int32, (width, side), 1)
        target[index // 2, :, 2 * KV_WIDTH :] = jnp.where(
            lane == 0, own_gain, jnp.where(lane == 1, gain[part, :], 0.0)
        ).astype(BF16)


def shards(
    tokens,
    cotangent,
    prenorm_scaling,
    hidden_gain,
    query_weight,
    key_matrix,
    value_matrix,
    output_weight,
    gate_weight,
    up_weight,
    down_weight,
):
    token_rows = tokens.shape[1]
    units = gate_weight.shape[1]
    ctx_size = lax.axis_size("ctx")
    ctx_me = lax.axis_index("ctx")
    tensor_me = lax.axis_index("tensor")
    scale_factor = ATTN_UNIT_DIM ** (-0.5)
    positions = (ctx_me * 2 + tensor_me) * token_rows + jnp.arange(token_rows, dtype=jnp.int32)
    cosine, sine = rotary_tables(positions)
    inputs = tokens[0].astype(F32)
    unrolled = ctx_size == 4

    side = jnp.stack([prenorm_scaling, hidden_gain], 1).astype(BF16)
    own_kv = jnp.concatenate([key_matrix, value_matrix, jnp.pad(side, ((0, 0), (0, 62)))], 1)
    own_ffn = jnp.concatenate([gate_weight, up_weight, down_weight.T], 1)
    far_kv = from_other_chips(own_kv)
    other_cotangent = swap_x(cotangent[0])
    inv_one = lax.rsqrt(jnp.mean(inputs * inputs, -1, keepdims=True) + EPS)
    far_kv, query_weight, inv_one = barrier((far_kv, query_weight, inv_one))
    far_query = from_other_chips(query_weight)
    kv_pieces = both_cores([own_kv] + far_kv)
    gains = in_order([piece[:, 2 * KV_WIDTH :] for piece in kv_pieces], 0).astype(F32).T
    gain_one, gain_two = gains[0], gains[1]
    places = jnp.stack(near_places()).astype(jnp.int32)

    normed_one = (inputs * inv_one * gain_one).astype(BF16)
    normed_one_turned = normed_one.T
    near_one = near_pieces(normed_one, 1)
    projected = sum(
        product(rows, weight[:, : 2 * KV_WIDTH], 1, 0) for weight, rows in zip(kv_pieces, near_one)
    )
    key_value = jnp.concatenate(
        [
            rotate_lanes(projected[:, :KV_WIDTH], cosine.T, sine.T).astype(BF16),
            projected[:, KV_WIDTH:].astype(BF16),
        ],
        1,
    )
    far_query, output_weight, other_cotangent = barrier(
        (far_query, output_weight, other_cotangent)
    )
    far_output = from_other_chips(output_weight)
    query_pieces = both_cores([query_weight] + far_query)
    query_projected = sum(
        product(weight, rows, 0, 1) for weight, rows in zip(query_pieces, near_one)
    )
    queries = to_lanes((rotate(query_projected, cosine, sine) * scale_factor).astype(BF16))
    later = tensor_me == 1
    flags = [(later if step == 0 else ctx_me >= step) for step in range(ctx_size)]
    passing = key_value
    tiles = [(key_value, swap_x(key_value))]
    stats, accum = forward_first(queries, key_value)
    for step in range(1, ctx_size):
        passing = shift_z(passing, 1)
        tiles.append((passing, swap_x(passing)))
    far_output, own_ffn, stats = barrier((far_output, own_ffn, stats))
    far_ffn = from_other_chips(own_ffn)
    stats, accum = forward_tiles(queries, [tiles[0][1]], [flags[0]], stats, accum)
    if unrolled:
        for step in range(1, ctx_size):
            stats, accum = forward_tiles(queries, tiles[step], [flags[step]] * 2, stats, accum)
    else:
        scanned = (
            jnp.stack([tile[0] for tile in tiles[1:]]),
            jnp.stack([tile[1] for tile in tiles[1:]]),
            jnp.stack(flags[1:]),
        )
        (stats, accum), unused = lax.scan(
            lambda held, item: (
                forward_tiles(queries, [item[0], item[1]], [item[2], item[2]], *held),
                None,
            ),
            (stats, accum),
            scanned,
        )

    output_pieces = both_cores([output_weight] + far_output)
    model = tokens.shape[2]
    attended, hidden_in, normed_two = on_core(
        functools.partial(mid_kernel, len(output_pieces)),
        "attended_to_normed",
        (
            ((Q_WIDTH, token_rows), BF16),
            ((token_rows, model), F32),
            ((token_rows, model), BF16),
        ),
        places,
        stats,
        accum,
        tokens[0],
        gain_two[None],
        *output_pieces,
        estimate=cost(2 * token_rows * Q_WIDTH * model, 8 * token_rows * model),
        scratch=[pltpu.VMEM((Q_WIDTH, model), BF16)],
        columns=model,
    )
    other_normed = swap_x(normed_two)
    far_ffn, own_ffn, normed_two = barrier((far_ffn, own_ffn, normed_two))
    ffn_pieces = both_cores([own_ffn] + far_ffn)
    unit_values, feed_own, feed_other, d_normed_own, d_normed_other = feed_forward(
        places,
        [normed_two, other_normed, cotangent[0], other_cotangent],
        ffn_pieces,
        units,
    )

    d_normed_came = swap_x(d_normed_other)
    ffn_kept, ffn_sent = feed_grads(
        places,
        [normed_two.T, other_normed.T, cotangent[0].T, other_cotangent.T],
        unit_values,
        units,
    )
    ffn_came = swap_core(ffn_sent)

    lanes = queries.shape[1]
    pieces_shape = (len(output_pieces) // 2, query_weight.shape[0])
    d_hidden, grads, stats, output_kept, output_sent, grad_gain_two = on_core(
        functools.partial(turn_kernel, len(output_pieces)),
        "normed_to_attended",
        (
            ((token_rows, model), F32),
            ((KV_WIDTH, lanes), BF16),
            ((16, lanes), F32),
            (pieces_shape + (model,), BF16),
            (pieces_shape + (model,), BF16),
            ((1, model), F32),
        ),
        places,
        d_normed_own,
        d_normed_came,
        hidden_in,
        cotangent[0],
        gain_two[None],
        attended,
        accum,
        stats,
        *output_pieces,
        estimate=cost(4 * token_rows * Q_WIDTH * model, 16 * token_rows * model),
        scratch=[pltpu.VMEM((Q_WIDTH, token_rows), BF16)],
        columns=model,
    )
    ffn_came, output_sent, d_query = barrier(
        (ffn_came, output_sent, jnp.zeros(accum.shape, F32))
    )

    def ffn_part(k):
        columns = slice(k * units, (k + 1) * units)
        return block_sums(ffn_kept[:, :, columns], ffn_came[:, :, columns])

    down_kept = ffn_part(0)
    down_came = chip_sends(down_kept)
    output_came = swap_core(output_sent)
    d_parts = {}
    if unrolled:
        for step in (3, 2):
            d_query, d_parts[step] = backward_tiles(
                queries, grads, stats, tiles[step], [flags[step]] * 2, d_query
            )
            if step == 3:
                pair_three = swap_x(d_parts[3][1])
    else:
        d_query, terms = lax.scan(
            lambda held, item: backward_tiles(
                queries, grads, stats, [item[0], item[1]], [item[2], item[2]], held
            ),
            d_query,
            scanned,
        )
        passing = None
        for step in reversed(range(1, ctx_size)):
            part = add_low(terms[0][step - 1], swap_x(terms[1][step - 1]))
            part = part if passing is None else add_low(part, passing)
            passing = shift_z(part, -1)
        pair_three = passing
    down_came, output_came, pair_three, d_query = barrier(
        (down_came, output_came, pair_three, d_query)
    )

    gate_kept = ffn_part(1)
    gate_came = chip_sends(gate_kept)
    down_sum = chip_sum(down_kept, down_came)
    down_came = line_in(down_sum)
    output_kept = block_sums(output_kept, output_came)
    passing = pair_three
    pair_one = pair_two = pair_three
    if unrolled:
        pair_two = swap_x(d_parts[2][1])
        passing = shift_z(add_low(d_parts[3][0], pair_three), -1)
        d_query, d_parts[1] = backward_tiles(
            queries, grads, stats, tiles[1], [flags[1]] * 2, d_query
        )
        pair_one = swap_x(d_parts[1][1])
    d_query, (pair_zero,) = backward_tiles(
        queries, grads, stats, [tiles[0][1]], [flags[0]], d_query
    )
    d_query, (own_zero,) = backward_tiles(
        queries, grads, stats, [key_value], [ctx_me >= 0], d_query, causal=True
    )
    gate_came, down_came, passing, pair_two, d_query, output_kept = barrier(
        (gate_came, down_came, passing, pair_two, d_query, output_kept)
    )

    up_kept = ffn_part(2)
    up_came = chip_sends(up_kept)
    gate_sum = chip_sum(gate_kept, gate_came)
    gate_came = line_in(gate_sum)
    down_half = line_half(down_sum, down_came)
    down_came = line_mid(down_half)
    if unrolled:
        passing = shift_z(add_low(add_low(d_parts[2][0], pair_two), passing), -1)
    pair_zero = swap_x(pair_zero)
    query_kept, query_sent, d_query_rows = on_core(
        functools.partial(query_kernel, len(query_pieces)),
        "query_grads",
        (
            (pieces_shape + (Q_WIDTH,), BF16),
            (pieces_shape + (Q_WIDTH,), BF16),
            ((model, token_rows), F32),
        ),
        places,
        d_query,
        cosine,
        sine,
        normed_one_turned,
        *query_pieces,
        estimate=cost(4 * token_rows * Q_WIDTH * model, 16 * token_rows * model),
        scratch=[pltpu.VMEM((Q_WIDTH, token_rows), BF16)],
        columns=Q_WIDTH,
    )
    query_came = swap_core(query_sent)
    up_came, gate_came, down_came, pair_one, passing, query_came = barrier(
        (up_came, gate_came, down_came, pair_one, passing, query_came)
    )

    up_sum = chip_sum(up_kept, up_came)
    up_came = line_in(up_sum)
    gate_half = line_half(gate_sum, gate_came)
    gate_came = line_mid(gate_half)
    down_total = line_total(down_half, down_came)
    down_came = line_out(down_total)
    query_kept = [
        jnp.concatenate([output, query], 1)
        for output, query in zip(output_kept, block_sums(query_kept, query_came))
    ]
    query_came = chip_sends(query_kept)
    if unrolled:
        passing = shift_z(add_low(add_low(d_parts[1][0], pair_one), passing), -1)

    last_kept, last_sent, d_rows = on_core(
        functools.partial(key_kernel, len(kv_pieces)),
        "key_value_grads",
        (
            (pieces_shape + (kv_pieces[0].shape[1],), BF16),
            (pieces_shape + (kv_pieces[0].shape[1],), BF16),
            ((model, token_rows), F32),
        ),
        places,
        own_zero,
        pair_zero,
        passing,
        cosine.T,
        sine.T,
        normed_one_turned,
        tokens[0].T,
        inv_one.T,
        d_query_rows,
        grad_gain_two.T,
        *kv_pieces,
        estimate=cost(4 * token_rows * 2 * KV_WIDTH * model, 16 * token_rows * model),
        scratch=[pltpu.VMEM((token_rows, 2 * KV_WIDTH), BF16)],
        columns=kv_pieces[0].shape[1],
    )
    last_came = swap_core(last_sent)
    up_came, gate_came, down_came, query_came, last_came, d_rows = barrier(
        (up_came, gate_came, down_came, query_came, last_came, d_rows)
    )

    last_kept = block_sums(last_kept, last_came)
    last_came = chip_sends(last_kept)
    query_mine, query_came = x_parts(chip_sum(query_kept, query_came))
    query_came = swap_x(query_came)
    up_half = line_half(up_sum, up_came)
    up_came = line_mid(up_half)
    gate_total = line_total(gate_half, gate_came)
    gate_came = line_out(gate_total)
    out_down = line_result(down_total, down_came).T.astype(F32)
    last_came, query_came, up_came, gate_came, out_down = barrier(
        (last_came, query_came, up_came, gate_came, out_down)
    )

    last_mine, last_came = x_parts(chip_sum(last_kept, last_came))
    last_came = swap_x(last_came)
    query_sum = add_low(query_mine, query_came)
    query_came = line_in(query_sum)
    up_total = line_total(up_half, up_came)
    up_came = line_out(up_total)
    d_normed_one = d_rows.T
    scaled_one = d_normed_one * gain_one
    d_inputs = (
        d_hidden
        + inv_one * scaled_one
        - inputs * inv_one**3 * jnp.mean(scaled_one * inputs, -1, keepdims=True)
    )
    out_gate = line_result(gate_total, gate_came).astype(F32)
    last_came, query_came, up_came, d_inputs, out_gate = barrier(
        (last_came, query_came, up_came, d_inputs, out_gate)
    )

    last_sum = add_low(last_mine, last_came)
    last_came = line_in(last_sum)
    query_half = line_half(query_sum, query_came)
    query_came = line_mid(query_half)
    feed_came = swap_x(feed_other)
    out_up = line_result(up_total, up_came).astype(F32)
    last_came, query_came, feed_came, out_up = barrier(
        (last_came, query_came, feed_came, out_up)
    )

    last_half = line_half(last_sum, last_came)
    last_came = line_mid(last_half)
    query_total = line_total(query_half, query_came)
    query_came = line_out(query_total)
    result = (hidden_in + feed_own + feed_came.astype(F32)).astype(BF16)[None]
    last_came, query_came, result = barrier((last_came, query_came, result))

    last_total = line_total(last_half, last_came)
    last_came = line_out(last_total)
    query_mine = line_result(query_total, query_came)
    query_came = swap_x(query_mine)
    last_came, query_came = barrier((last_came, query_came))
    joined = x_join(query_mine, query_came)
    last_mine = line_result(last_total, last_came)
    last = x_join(last_mine, swap_x(last_mine))
    return (
        result,
        d_inputs[None],
        last[:, 2 * KV_WIDTH],
        last[:, 2 * KV_WIDTH + 1],
        joined[:, output_weight.shape[1] :],
        last[:, :KV_WIDTH],
        last[:, KV_WIDTH : 2 * KV_WIDTH],
        joined[:, : output_weight.shape[1]],
        out_gate,
        out_up,
        out_down,
    )


def solution(mesh):
    return jax.shard_map(
        shards,
        mesh=mesh,
        in_specs=(
            P("shard", ("ctx", "tensor"), None),
            P("shard", ("ctx", "tensor"), None),
            P("shard"),
            P("shard"),
            P("shard", None),
            P("shard", None),
            P("shard", None),
            P("shard", None),
            P("shard", "tensor"),
            P("shard", "tensor"),
            P("tensor", "shard"),
        ),
        out_specs=(
            P("shard", ("ctx", "tensor"), None),
            P("shard", ("ctx", "tensor"), None),
            P("shard"),
            P("shard"),
            P("shard", None),
            P("shard", None),
            P("shard", None),
            P("shard", None),
            P("shard", "tensor"),
            P("shard", "tensor"),
            P("tensor", "shard"),
        ),
        check_vma=False,
    )
```

```python
import functools

import jax
import jax.numpy as jnp
from jax import lax
from jax.experimental import pallas as pl
from jax.experimental.pallas import tpu as pltpu
from jax.sharding import PartitionSpec as P

QUERY_HEADS = 15
SHARED_KV_UNITS = 5
ATTN_UNIT_DIM = 64
GROUP = QUERY_HEADS // SHARED_KV_UNITS
KV_WIDTH = SHARED_KV_UNITS * ATTN_UNIT_DIM
Q_WIDTH = QUERY_HEADS * ATTN_UNIT_DIM

EPS = 1e-05
THETA = 100000.0
F32 = jnp.float32
BF16 = jnp.bfloat16
barrier = lax.optimization_barrier


def rotary_tables(positions):
    half = ATTN_UNIT_DIM // 2
    freqs = THETA ** (-(jnp.arange(half, dtype=F32) * 2.0 / ATTN_UNIT_DIM))
    angles = freqs[:, None] * positions.astype(F32)[None, :]
    return (jnp.cos(angles), jnp.sin(angles))


def rotate(block, cosine, sine):
    split = block.reshape(-1, 2, ATTN_UNIT_DIM // 2, block.shape[1])
    former, latter = split[:, 0], split[:, 1]
    turned = jnp.stack([former * cosine - latter * sine, latter * cosine + former * sine], 1)
    return turned.reshape(block.shape)


def rotate_lanes(block, cosine, sine):
    split = block.reshape(block.shape[0], -1, 2, ATTN_UNIT_DIM // 2)
    former, latter = split[:, :, 0], split[:, :, 1]
    cosine, sine = cosine[:, None, :], sine[:, None, :]
    turned = jnp.stack([former * cosine - latter * sine, latter * cosine + former * sine], 2)
    return turned.reshape(block.shape)


def product(left, right, left_dim, right_dim):
    return lax.dot_general(
        left, right, (((left_dim,), (right_dim,)), ((), ())), preferred_element_type=F32
    )


def swap_core(block):
    size = lax.axis_size("shard")
    return lax.ppermute(block, "shard", [(i, i ^ 1) for i in range(size)])


def shift_y(block, step):
    size = lax.axis_size("shard")
    return lax.ppermute(block, "shard", [(i, (i + 2 * step) % size) for i in range(size)])


def swap_x(block):
    return lax.ppermute(block, "tensor", [(0, 1), (1, 0)])


def shift_z(block, step):
    size = lax.axis_size("ctx")
    pairs = [(i, i + step) for i in range(size) if 0 <= i + step < size]
    return lax.ppermute(block, "ctx", pairs)


def from_other_chips(own):
    return [shift_y(own, -step) for step in range(1, lax.axis_size("shard") // 2)]


def both_cores(held):
    return [piece for block in held for piece in (block, swap_core(block))]


def near_places():
    size = lax.axis_size("shard")
    me = lax.axis_index("shard")
    places = []
    for step in range(size // 2):
        owner = lax.rem(me + 2 * step, size)
        places += [owner, jnp.bitwise_xor(owner, 1)]
    return places


def near_pieces(whole, dim):
    width = whole.shape[dim] // lax.axis_size("shard")
    return [lax.dynamic_slice_in_dim(whole, p * width, width, dim) for p in near_places()]


def in_order(pieces, dim):
    places = near_places()
    ordered = []
    for index in range(len(pieces)):
        piece = pieces[0]
        for place, other in zip(places[1:], pieces[1:]):
            piece = jnp.where(place == index, other, piece)
        ordered.append(piece)
    return jnp.concatenate(ordered, dim)


def add_low(left, right):
    return (left.astype(F32) + right.astype(F32)).astype(BF16)


def block_sums(kept, came):
    return [add_low(kept[step], came[step]) for step in range(kept.shape[0])]


def chip_sends(kept):
    return [shift_y(block, step) for step, block in enumerate(kept) if step > 0]


def chip_sum(kept, came):
    total = kept[0].astype(F32)
    for block in came:
        total = total + block.astype(F32)
    return total.astype(BF16)


def on_line():
    return lax.axis_size("ctx") == 4


def line_in(block):
    return lax.ppermute(block, "ctx", [(0, 1), (3, 2)]) if on_line() else block


def line_mid(half):
    return lax.ppermute(half, "ctx", [(1, 2), (2, 1)]) if on_line() else half


def line_out(total):
    return lax.ppermute(total, "ctx", [(1, 0), (2, 3)]) if on_line() else total


def line_half(block, came):
    return add_low(block, came) if on_line() else lax.psum(block, "ctx")


def line_total(half, came):
    return add_low(half, came) if on_line() else half


def line_result(total, came):
    if not on_line():
        return total
    me = lax.axis_index("ctx")
    return jnp.where(jnp.logical_or(me == 1, me == 2), total, came)


def x_parts(block):
    half = block.shape[0] // 2
    me = lax.axis_index("tensor")
    kept = lax.dynamic_slice_in_dim(block, me * half, half, 0)
    sent = lax.dynamic_slice_in_dim(block, (1 - me) * half, half, 0)
    return kept, sent


def x_join(block, other):
    first = lax.axis_index("tensor") == 0
    return jnp.concatenate(
        [jnp.where(first, block, other), jnp.where(first, other, block)], 0
    ).astype(F32)


def head_part(head, offset=0):
    return slice(offset + head * ATTN_UNIT_DIM, offset + (head + 1) * ATTN_UNIT_DIM)


def causal_mask(keys, lanes, rows):
    key = lax.broadcasted_iota(jnp.int32, (keys, lanes), 0)
    lane = lax.broadcasted_iota(jnp.int32, (keys, lanes), 1)
    return key <= lax.rem(lane, rows)


def forward_first_kernel(query_ref, tile_ref, stats_ref, accum_ref):
    rows = tile_ref.shape[0]
    lanes = query_ref.shape[1]
    mask = causal_mask(rows, lanes, rows)
    stats_ref[...] = jnp.zeros_like(stats_ref)
    for head in range(SHARED_KV_UNITS):
        key = tile_ref[:, head_part(head)]
        value = tile_ref[:, head_part(head, KV_WIDTH)]
        scores = jnp.dot(key, query_ref[head_part(head), :], preferred_element_type=F32)
        scores = jnp.where(mask, scores, -1e30)
        peak = jnp.max(scores, 0, keepdims=True)
        probs = jnp.exp(scores - peak)
        stats_ref[head : head + 1, :] = peak
        stats_ref[8 + head : 9 + head, :] = jnp.sum(probs, 0, keepdims=True)
        accum_ref[head_part(head), :] = product(value, probs.astype(BF16), 0, 0)


def forward_kernel(count, flags_ref, query_ref, *refs):
    tiles, (stats_in, accum_in, stats_ref, accum_ref) = refs[:count], refs[count:]
    stats_ref[...] = stats_in[...]
    accum_ref[...] = accum_in[...]
    for index, tile_ref in enumerate(tiles):

        @pl.when(flags_ref[index] != 0)
        def _(tile_ref=tile_ref):
            for head in range(SHARED_KV_UNITS):
                key = tile_ref[:, head_part(head)]
                value = tile_ref[:, head_part(head, KV_WIDTH)]
                scores = jnp.dot(key, query_ref[head_part(head), :], preferred_element_type=F32)
                old_peak = stats_ref[head : head + 1, :]
                peak = jnp.maximum(old_peak, jnp.max(scores, 0, keepdims=True))
                probs = jnp.exp(scores - peak)
                rescale = jnp.exp(old_peak - peak)
                total = stats_ref[8 + head : 9 + head, :]
                stats_ref[head : head + 1, :] = peak
                stats_ref[8 + head : 9 + head, :] = total * rescale + jnp.sum(
                    probs, 0, keepdims=True
                )
                accum_ref[head_part(head), :] = accum_ref[head_part(head), :] * rescale + (
                    product(value, probs.astype(BF16), 0, 0)
                )


def backward_kernel(causal, count, flags_ref, query_ref, grad_ref, stats_ref, *refs):
    tiles, (into, out_ref), sums = refs[:count], refs[count : count + 2], refs[count + 2 :]
    if len(sums) < count:
        sums = (sums[0], sums[1].at[0], sums[1].at[1])
    rows = tiles[0].shape[0]
    lanes = query_ref.shape[1]
    out_ref[...] = into[...]
    for index, (tile_ref, sum_ref) in enumerate(zip(tiles, sums)):

        @pl.when(flags_ref[index] == 0)
        def _(sum_ref=sum_ref):
            sum_ref[...] = jnp.zeros_like(sum_ref)

        @pl.when(flags_ref[index] != 0)
        def _(tile_ref=tile_ref, sum_ref=sum_ref):
            for head in range(SHARED_KV_UNITS):
                key = tile_ref[:, head_part(head)]
                value = tile_ref[:, head_part(head, KV_WIDTH)]
                query = query_ref[head_part(head), :]
                grad = grad_ref[head_part(head), :]
                scores = jnp.dot(key, query, preferred_element_type=F32)
                probs = jnp.exp(scores - stats_ref[head : head + 1, :])
                if causal:
                    probs = jnp.where(causal_mask(rows, lanes, rows), probs, 0.0)
                d_probs = jnp.dot(value, grad, preferred_element_type=F32)
                d_scores = (probs * (d_probs - stats_ref[8 + head : 9 + head, :])).astype(BF16)
                sum_ref[:, head_part(head)] = product(d_scores, query, 1, 1).astype(BF16)
                sum_ref[:, head_part(head, KV_WIDTH)] = product(
                    probs.astype(BF16), grad, 1, 1
                ).astype(BF16)
                out_ref[head_part(head), :] += product(key, d_scores, 0, 0)


def cost(multiply_adds, values=0, transcendentals=0):
    return pl.CostEstimate(
        flops=2 * multiply_adds, bytes_accessed=values, transcendentals=transcendentals
    )


def tile_cost(count, rows, lanes, matmuls):
    return cost(
        4 * matmuls * count * rows * lanes * KV_WIDTH,
        8 * KV_WIDTH * lanes,
        count * rows * lanes * SHARED_KV_UNITS,
    )


MEMORY = pltpu.CompilerParams(vmem_limit_bytes=24 * 1024 * 1024)
LARGE = pltpu.CompilerParams(vmem_limit_bytes=58 * 1024 * 1024)
IN_VMEM = pl.BlockSpec(memory_space=pltpu.VMEM)
IN_SMEM = pl.BlockSpec(memory_space=pltpu.SMEM)


def on_core(
    kernel, name, out_shape, *operands, estimate, scratch=(), first_in_smem=True, columns=None
):
    def block(shape):
        return pl.BlockSpec(shape, lambda i: (0,) * len(shape))

    specs = [IN_VMEM] * len(operands)
    outs = [IN_VMEM] * len(out_shape)
    if columns is not None:
        last = operands[-1].shape
        specs = [
            block((last[0], columns) if operand.shape == last else operand.shape)
            for operand in operands
        ]
        outs = [block(shape[0]) for shape in out_shape]
    if first_in_smem:
        specs[0] = IN_SMEM
    return pl.pallas_call(
        kernel,
        grid=() if columns is None else (1,),
        in_specs=specs,
        out_specs=tuple(outs),
        out_shape=tuple(jax.ShapeDtypeStruct(*shape) for shape in out_shape),
        scratch_shapes=list(scratch),
        cost_estimate=estimate,
        compiler_params=MEMORY if columns is None else LARGE,
        name=name,
    )(*operands)


def forward_first(query, tile):
    lanes = query.shape[1]
    return on_core(
        forward_first_kernel,
        "attend_own",
        (((16, lanes), F32), ((KV_WIDTH, lanes), F32)),
        query,
        tile,
        estimate=tile_cost(1, tile.shape[0], lanes, 2),
        first_in_smem=False,
    )


def forward_tiles(query, tiles, flags, stats, accum):
    return on_core(
        functools.partial(forward_kernel, len(tiles)),
        "attend",
        ((stats.shape, F32), (accum.shape, F32)),
        jnp.stack(flags).astype(jnp.int32),
        query,
        *tiles,
        stats,
        accum,
        estimate=tile_cost(len(tiles), tiles[0].shape[0], query.shape[1], 2),
    )


def backward_tiles(query, grad, stats, tiles, flags, into, causal=False):
    shape = tiles[0].shape
    sums = (shape, (2,) + shape) if len(tiles) == 3 else (shape,) * len(tiles)
    out = on_core(
        functools.partial(backward_kernel, causal, len(tiles)),
        "attend_back",
        ((into.shape, F32),) + tuple((item, BF16) for item in sums),
        jnp.stack(flags).astype(jnp.int32),
        query,
        grad,
        stats,
        *tiles,
        into,
        estimate=tile_cost(len(tiles), tiles[0].shape[0], query.shape[1], 20),
    )
    return out[0], out[1:]


def to_lanes(block):
    rows = block.shape[1]
    split = block.reshape(SHARED_KV_UNITS, GROUP, ATTN_UNIT_DIM, rows)
    return split.transpose(0, 2, 1, 3).reshape(KV_WIDTH, GROUP * rows)


def place_rows(places, index, width):
    return pl.ds(pl.multiple_of(places[index] * width, 16), width)


def put_in_order(places, pieces, whole, columns):
    width = pieces[0].shape[0]
    for index, piece in enumerate(pieces):
        whole[place_rows(places, index, width), :] = piece[:, :columns]


def mid_kernel(count, places, stats, accum, inputs, gain, *refs):
    weights = refs[:count]
    attended_ref, hidden_ref, normed_ref, weight = refs[count:]
    rows, model = inputs.shape
    put_in_order(places, weights, weight, model)
    for head in range(SHARED_KV_UNITS):
        part = accum[head_part(head), :] / stats[8 + head : 9 + head, :]
        for member in range(GROUP):
            attended_ref[head_part(head * GROUP + member), :] = part[
                :, member * rows : (member + 1) * rows
            ].astype(BF16)
    hidden = inputs[...].astype(F32) + product(attended_ref[...], weight[...], 0, 0)
    hidden_ref[...] = hidden
    inverse = lax.rsqrt(jnp.mean(hidden * hidden, -1, keepdims=True) + EPS)
    normed_ref[:, :model] = (hidden * inverse * gain[...]).astype(BF16)
    normed_ref[:, model:] = jnp.zeros((rows, normed_ref.shape[1] - model), BF16)


def feed_kernel(count, places, *refs):
    normed_own, normed_other, upstream_own, upstream_other = refs[:4]
    gates, ups, downs = (refs[4 + k * count : 4 + (k + 1) * count] for k in range(3))
    units_ref, turned, feed_own, feed_other, grad_own, grad_other = refs[
        4 + 3 * count : 10 + 3 * count
    ]
    gate, up, down, normed, upstream, feed_sum, grad_sum = refs[10 + 3 * count :]
    rows = normed_own.shape[0]
    model, tile = gate.shape

    @pl.when(pl.program_id(0) == 0)
    def _():
        normed[:rows, :] = normed_own[...]
        normed[rows:, :] = normed_other[...]
        turned[...] = normed[...].T
        upstream[:rows, :] = upstream_own[...]
        upstream[rows:, :] = upstream_other[...]
        feed_sum[...] = jnp.zeros_like(feed_sum)
        grad_sum[...] = jnp.zeros_like(grad_sum)

    for pieces, whole in ((gates, gate), (ups, up), (downs, down)):
        put_in_order(places, pieces, whole, tile)
    gate_val = jnp.dot(normed[:, :model], gate[...], preferred_element_type=F32)
    up_val = jnp.dot(normed[:, :model], up[...], preferred_element_type=F32)
    d_product = jnp.dot(upstream[...], down[...], preferred_element_type=F32)
    sigmoid = 0.5 * jnp.tanh(0.5 * gate_val) + 0.5
    silu = gate_val * sigmoid
    z = (silu * up_val).astype(BF16)
    d_up = (d_product * silu).astype(BF16)
    d_gate = (d_product * up_val * sigmoid * (1.0 + gate_val * (1.0 - sigmoid))).astype(BF16)
    units_ref[:, :tile] = z
    units_ref[:, tile : 2 * tile] = d_gate
    units_ref[:, 2 * tile :] = d_up
    grad_sum[...] += product(d_gate, gate[...], 1, 1) + product(d_up, up[...], 1, 1)
    feed_sum[...] += product(z, down[...], 1, 1)

    @pl.when(pl.program_id(0) == pl.num_programs(0) - 1)
    def _():
        for total, own, other in ((feed_sum, feed_own, feed_other), (grad_sum, grad_own, grad_other)):
            own[...] = total[:rows, :]
            other[...] = total[rows:, :].astype(BF16)


def feed_tile(units):
    return units // 2


def feed_forward(places, rows_in, packed, units):
    count = len(packed)
    rows, wide = rows_in[0].shape
    model = rows_in[2].shape[1]
    width = packed[0].shape[0]
    tile = feed_tile(units)
    steps = units // tile
    whole = pl.BlockSpec((rows, model), lambda i: (0, 0))
    wide_spec = pl.BlockSpec((rows, wide), lambda i: (0, 0))
    gate_spec = pl.BlockSpec((width, tile), lambda i: (0, i))
    up_spec = pl.BlockSpec((width, tile), lambda i: (0, i + steps))
    down_spec = pl.BlockSpec((width, tile), lambda i: (0, i + 2 * steps))
    out_spec = pl.BlockSpec((2 * rows, 3 * tile), lambda i: (0, i))
    return pl.pallas_call(
        functools.partial(feed_kernel, count),
        grid=(steps,),
        in_specs=[IN_SMEM, wide_spec, wide_spec, whole, whole]
        + [gate_spec] * count
        + [up_spec] * count
        + [down_spec] * count,
        out_specs=(out_spec, pl.BlockSpec((wide, 2 * rows), lambda i: (0, 0))) + (whole,) * 4,
        out_shape=(
            jax.ShapeDtypeStruct((2 * rows, 3 * units), BF16),
            jax.ShapeDtypeStruct((wide, 2 * rows), BF16),
        )
        + (
            jax.ShapeDtypeStruct((rows, model), F32),
            jax.ShapeDtypeStruct((rows, model), BF16),
        )
        * 2,
        scratch_shapes=[pltpu.VMEM((model, tile), BF16)] * 3
        + [pltpu.VMEM((2 * rows, wide), BF16), pltpu.VMEM((2 * rows, model), BF16)]
        + [pltpu.VMEM((2 * rows, model), F32)] * 2,
        cost_estimate=cost(12 * rows * model * units, 6 * model * units, rows * units),
        compiler_params=LARGE,
        name="feed_forward",
    )(places, *rows_in, *packed, *packed, *packed)


def grad_kernel(count, width, places, turned, values, kept, sent):
    for index in range(count):
        total = jnp.dot(
            turned[place_rows(places, index, width), :], values[...], preferred_element_type=F32
        )
        (kept, sent)[index % 2][index // 2] = total.astype(BF16)


def feed_grads(places, turned, values, units, model, which):
    count = lax.axis_size("shard")
    rows = turned.shape[1]
    width = model // count
    tile = feed_tile(units)
    whole = pl.BlockSpec(turned.shape, lambda i: (0, 0))
    sum_spec = pl.BlockSpec((count // 2, width, tile), lambda i: (0, 0, i))
    return pl.pallas_call(
        functools.partial(grad_kernel, count, width),
        grid=(units // tile,),
        in_specs=[IN_SMEM, whole, pl.BlockSpec((rows, tile), lambda i: (0, 3 * i + which))],
        out_specs=(sum_spec,) * 2,
        out_shape=(jax.ShapeDtypeStruct((count // 2, width, units), BF16),) * 2,
        cost_estimate=cost(2 * rows * model * units, 4 * model * units),
        compiler_params=LARGE,
        name="feed_grads",
    )(places, turned, values)


def turn_kernel(count, places, *refs):
    own, came, hidden_ref, upstream, gain, attended, accum, stats = refs[:8]
    weights = refs[8 : 8 + count]
    d_hidden_ref, grads, stats_ref, kept, sent, gain_ref, turned = refs[8 + count :]
    rows, model = hidden_ref.shape
    width = weights[0].shape[0]
    hidden = hidden_ref[...]
    d_normed = own[...] + came[...].astype(F32)
    inverse = lax.rsqrt(jnp.mean(hidden * hidden, -1, keepdims=True) + EPS)
    gain_ref[...] = jnp.sum(d_normed * hidden * inverse, 0, keepdims=True)
    scaled = d_normed * gain[...]
    d_hidden = (
        upstream[...].astype(F32)
        + inverse * scaled
        - hidden * (inverse * inverse * inverse * jnp.mean(scaled * hidden, -1, keepdims=True))
    )
    d_hidden_ref[...] = d_hidden
    d_branch = d_hidden.astype(BF16)
    for index, weight in enumerate(weights):
        part = place_rows(places, index, width)
        turned[part, :] = product(weight[:, :model], d_branch, 1, 1).astype(BF16)
        (kept, sent)[index % 2][index // 2] = jnp.dot(
            attended[part, :], d_branch, preferred_element_type=F32
        ).astype(BF16)
    stats_ref[...] = jnp.zeros_like(stats_ref)
    for head in range(SHARED_KV_UNITS):
        for member in range(GROUP):
            lanes = slice(member * rows, (member + 1) * rows)
            grads[head_part(head), lanes] = turned[head_part(head * GROUP + member), :]
        total = stats[8 + head : 9 + head, :]
        stats_ref[head : head + 1, :] = stats[head : head + 1, :] + jnp.log(total)
        stats_ref[8 + head : 9 + head, :] = jnp.sum(
            grads[head_part(head), :].astype(F32) * (accum[head_part(head), :] / total),
            0,
            keepdims=True,
        )


def query_kernel(count, places, d_query, cosine, sine, normed, *refs):
    weights = refs[:count]
    kept, sent, d_rows, turned = refs[count:]
    rows = normed.shape[1]
    width = weights[0].shape[0]
    half = ATTN_UNIT_DIM // 2
    scale = ATTN_UNIT_DIM ** (-0.5)
    for head in range(SHARED_KV_UNITS):
        for member in range(GROUP):
            lanes = slice(member * rows, (member + 1) * rows)
            start = head * ATTN_UNIT_DIM
            former = d_query[start : start + half, lanes] * scale
            latter = d_query[start + half : start + 2 * half, lanes] * scale
            start = (head * GROUP + member) * ATTN_UNIT_DIM
            turned[start : start + half, :] = (
                former * cosine[...] + latter * sine[...]
            ).astype(BF16)
            turned[start + half : start + 2 * half, :] = (
                latter * cosine[...] - former * sine[...]
            ).astype(BF16)
    for index, weight in enumerate(weights):
        part = place_rows(places, index, width)
        (kept, sent)[index % 2][index // 2] = product(normed[part, :], turned[...], 1, 1).astype(
            BF16
        )
        d_rows[part, :] = jnp.dot(weight[...], turned[...], preferred_element_type=F32)


def key_kernel(count, places, *refs):
    own, pair, passing, cosine, sine, normed, inputs, inverse, d_query_rows, gain = refs[:10]
    weights = refs[10 : 10 + count]
    kept, sent, d_rows, turned = refs[10 + count :]
    width = weights[0].shape[0]
    half = ATTN_UNIT_DIM // 2
    total = own[...].astype(F32) + pair[...].astype(F32) + passing[...].astype(F32)
    for head in range(SHARED_KV_UNITS):
        start = head * ATTN_UNIT_DIM
        former = total[:, start : start + half]
        latter = total[:, start + half : start + 2 * half]
        turned[:, start : start + half] = (former * cosine[...] + latter * sine[...]).astype(BF16)
        turned[:, start + half : start + 2 * half] = (
            latter * cosine[...] - former * sine[...]
        ).astype(BF16)
    turned[:, KV_WIDTH:] = total[:, KV_WIDTH:].astype(BF16)
    for index, weight in enumerate(weights):
        part = place_rows(places, index, width)
        d_part = d_query_rows[part, :] + product(weight[:, : 2 * KV_WIDTH], turned[...], 1, 1)
        d_rows[part, :] = d_part
        own_gain = jnp.sum(
            d_part * inputs[part, :].astype(F32) * inverse[...], 1, keepdims=True
        )
        target = (kept, sent)[index % 2]
        target[index // 2, :, : 2 * KV_WIDTH] = jnp.dot(
            normed[part, :], turned[...], preferred_element_type=F32
        ).astype(BF16)
        side = target.shape[2] - 2 * KV_WIDTH
        lane = lax.broadcasted_iota(jnp.int32, (width, side), 1)
        target[index // 2, :, 2 * KV_WIDTH :] = jnp.where(
            lane == 0, own_gain, jnp.where(lane == 1, gain[part, :], 0.0)
        ).astype(BF16)


def shards(
    tokens,
    cotangent,
    prenorm_scaling,
    hidden_gain,
    query_weight,
    key_matrix,
    value_matrix,
    output_weight,
    gate_weight,
    up_weight,
    down_weight,
):
    token_rows = tokens.shape[1]
    units = gate_weight.shape[1]
    ctx_size = lax.axis_size("ctx")
    ctx_me = lax.axis_index("ctx")
    tensor_me = lax.axis_index("tensor")
    scale_factor = ATTN_UNIT_DIM ** (-0.5)
    positions = (ctx_me * 2 + tensor_me) * token_rows + jnp.arange(token_rows, dtype=jnp.int32)
    cosine, sine = rotary_tables(positions)
    inputs = tokens[0].astype(F32)
    unrolled = ctx_size == 4

    side = jnp.stack([prenorm_scaling, hidden_gain], 1).astype(BF16)
    own_kv = jnp.concatenate([key_matrix, value_matrix, jnp.pad(side, ((0, 0), (0, 126)))], 1)
    far_kv = from_other_chips(own_kv)
    other_cotangent = swap_x(cotangent[0])
    inv_one = lax.rsqrt(jnp.mean(inputs * inputs, -1, keepdims=True) + EPS)
    far_kv, query_weight, inv_one, tokens_turned = barrier(
        (far_kv, query_weight, inv_one, tokens[0].T)
    )
    far_query = from_other_chips(query_weight)
    kv_pieces = both_cores([own_kv] + far_kv)
    gains = in_order([piece[:, 2 * KV_WIDTH :] for piece in kv_pieces], 0).astype(F32).T
    gain_one, gain_two = gains[0], gains[1]
    places = jnp.stack(near_places()).astype(jnp.int32)

    normed_one = (inputs * inv_one * gain_one).astype(BF16)
    normed_one_turned = normed_one.T
    near_one = near_pieces(normed_one, 1)
    projected = sum(
        product(rows, weight[:, : 2 * KV_WIDTH], 1, 0) for weight, rows in zip(kv_pieces, near_one)
    )
    key_value = jnp.concatenate(
        [
            rotate_lanes(projected[:, :KV_WIDTH], cosine.T, sine.T).astype(BF16),
            projected[:, KV_WIDTH:].astype(BF16),
        ],
        1,
    )
    far_query, output_weight, other_cotangent, gate_weight = barrier(
        (far_query, output_weight, other_cotangent, gate_weight)
    )
    turned_upstream = jnp.concatenate([cotangent[0], other_cotangent], 0).T
    own_ffn = jnp.concatenate([gate_weight, up_weight, down_weight.T], 1)
    far_output = from_other_chips(output_weight)
    query_pieces = both_cores([query_weight] + far_query)
    query_projected = sum(
        product(weight, rows, 0, 1) for weight, rows in zip(query_pieces, near_one)
    )
    queries = to_lanes((rotate(query_projected, cosine, sine) * scale_factor).astype(BF16))
    later = tensor_me == 1
    flags = [(later if step == 0 else ctx_me >= step) for step in range(ctx_size)]
    passing = key_value
    passing = shift_z(key_value, 1)
    pair_zero = swap_x(key_value)
    stats, accum = forward_first(queries, key_value)
    pair_one, after = swap_x(passing), shift_z(passing, 1)
    stats, accum = forward_tiles(queries, [pair_zero], [flags[0]], stats, accum)
    far_output, own_ffn, stats, pair_one, after = barrier(
        (far_output, own_ffn, stats, pair_one, after)
    )
    far_ffn = from_other_chips(own_ffn)
    tiles = [(key_value, pair_zero), (passing, pair_one), (after, swap_x(after))]
    if unrolled:
        stats, accum = forward_tiles(queries, tiles[1], [flags[1]] * 2, stats, accum)
        after, stats = barrier((shift_z(after, 1), stats))
        tiles.append((after, swap_x(after)))
    for step in range(3, 3 if unrolled else ctx_size):
        after = shift_z(after, 1)
        tiles.append((after, swap_x(after)))
    if unrolled:
        for step in range(2, ctx_size):
            stats, accum = forward_tiles(queries, tiles[step], [flags[step]] * 2, stats, accum)
    else:
        scanned = (
            jnp.stack([tile[0] for tile in tiles[1:]]),
            jnp.stack([tile[1] for tile in tiles[1:]]),
            jnp.stack(flags[1:]),
        )
        (stats, accum), unused = lax.scan(
            lambda held, item: (
                forward_tiles(queries, [item[0], item[1]], [item[2], item[2]], *held),
                None,
            ),
            (stats, accum),
            scanned,
        )

    output_pieces = both_cores([output_weight] + far_output)
    model = tokens.shape[2]
    wide = -(-model // 128) * 128
    attended, hidden_in, normed_two = on_core(
        functools.partial(mid_kernel, len(output_pieces)),
        "attended_to_normed",
        (
            ((Q_WIDTH, token_rows), BF16),
            ((token_rows, model), F32),
            ((token_rows, wide), BF16),
        ),
        places,
        stats,
        accum,
        tokens[0],
        gain_two[None],
        *output_pieces,
        estimate=cost(2 * token_rows * Q_WIDTH * model, 8 * token_rows * model),
        scratch=[pltpu.VMEM((Q_WIDTH, model), BF16)],
        columns=model,
    )
    other_normed = swap_x(normed_two)
    near_ffn = swap_core(own_ffn)
    other_normed, far_ffn, near_ffn = barrier((other_normed, far_ffn, near_ffn))
    ffn_pieces = [own_ffn, near_ffn] + both_cores(far_ffn)
    unit_values, turned, feed_own, feed_other, d_normed_own, d_normed_other = feed_forward(
        places,
        [normed_two, other_normed, cotangent[0], other_cotangent],
        ffn_pieces,
        units,
    )

    d_normed_came = swap_x(d_normed_other)
    kept_down, down_sent = feed_grads(places, turned_upstream, unit_values, units, model, 0)
    kept_gate, gate_sent = feed_grads(places, turned, unit_values, units, model, 1)
    kept_up, up_sent = feed_grads(places, turned, unit_values, units, model, 2)
    down_came = swap_core(down_sent)
    gate_came = swap_core(gate_sent)
    up_came = swap_core(up_sent)

    lanes = queries.shape[1]
    pieces_shape = (len(output_pieces) // 2, query_weight.shape[0])
    d_hidden, grads, stats, output_kept, output_sent, grad_gain_two = on_core(
        functools.partial(turn_kernel, len(output_pieces)),
        "normed_to_attended",
        (
            ((token_rows, model), F32),
            ((KV_WIDTH, lanes), BF16),
            ((16, lanes), F32),
            (pieces_shape + (model,), BF16),
            (pieces_shape + (model,), BF16),
            ((1, model), F32),
        ),
        places,
        d_normed_own,
        d_normed_came,
        hidden_in,
        cotangent[0],
        gain_two[None],
        attended,
        accum,
        stats,
        *output_pieces,
        estimate=cost(40 * token_rows * Q_WIDTH * model, 16 * token_rows * model),
        scratch=[pltpu.VMEM((Q_WIDTH, token_rows), BF16)],
        columns=model,
    )
    output_sent, down_came, gate_came, d_query = barrier(
        (output_sent, down_came, gate_came, jnp.zeros(accum.shape, F32))
    )
    down_kept = block_sums(kept_down, down_came)
    down_came = chip_sends(down_kept)
    gate_kept = block_sums(kept_gate, gate_came)
    gate_came = chip_sends(gate_kept)

    output_came = swap_core(output_sent)
    d_parts = {}
    if unrolled:
        d_query, d_parts[3] = backward_tiles(
            queries, grads, stats, tiles[3], [flags[3]] * 2, d_query
        )
        pair_three = swap_x(d_parts[3][1])
    else:
        d_query, terms = lax.scan(
            lambda held, item: backward_tiles(
                queries, grads, stats, [item[0], item[1]], [item[2], item[2]], held
            ),
            d_query,
            scanned,
        )
        passing = None
        for step in reversed(range(1, ctx_size)):
            part = add_low(terms[0][step - 1], swap_x(terms[1][step - 1]))
            part = part if passing is None else add_low(part, passing)
            passing = shift_z(part, -1)
        pair_three = passing
    down_came, d_query = barrier((down_came, d_query))
    down_sum = chip_sum(down_kept, down_came)
    down_came = line_in(down_sum)
    if unrolled:
        d_query, d_parts[2] = backward_tiles(
            queries, grads, stats, tiles[2], [flags[2]] * 2, d_query
        )
    up_came, output_came, pair_three, d_query = barrier(
        (up_came, output_came, pair_three, d_query)
    )

    up_kept = block_sums(kept_up, up_came)
    up_came = chip_sends(up_kept)
    output_kept = block_sums(output_kept, output_came)
    passing = pair_three
    pair_two = pair_three
    if unrolled:
        pair_two = swap_x(d_parts[2][1])
        passing = shift_z(add_low(d_parts[3][0], pair_three), -1)
        d_query, (own_one, pairs) = backward_tiles(
            queries,
            grads,
            stats,
            [tiles[1][0], tiles[1][1], tiles[0][1]],
            [flags[1], flags[1], flags[0]],
            d_query,
        )
        pair_two, passing, gate_came, down_came, d_query = barrier(
            (pair_two, passing, gate_came, down_came, d_query)
        )
        passing = shift_z(add_low(add_low(d_parts[2][0], pair_two), passing), -1)
    else:
        d_query, (pairs,) = backward_tiles(
            queries, grads, stats, [tiles[0][1]], [flags[0]], d_query
        )
    d_query, (own_zero,) = backward_tiles(
        queries, grads, stats, [key_value], [ctx_me >= 0], d_query, causal=True
    )
    gate_sum = chip_sum(gate_kept, gate_came)
    gate_came = line_in(gate_sum)
    down_half = line_half(down_sum, down_came)
    down_came = line_mid(down_half)
    pairs = swap_x(pairs)
    query_kept, query_sent, d_query_rows = on_core(
        functools.partial(query_kernel, len(query_pieces)),
        "query_grads",
        (
            (pieces_shape + (Q_WIDTH,), BF16),
            (pieces_shape + (Q_WIDTH,), BF16),
            ((model, token_rows), F32),
        ),
        places,
        d_query,
        cosine,
        sine,
        normed_one_turned,
        *query_pieces,
        estimate=cost(4 * token_rows * Q_WIDTH * model, 16 * token_rows * model),
        scratch=[pltpu.VMEM((Q_WIDTH, token_rows), BF16)],
        columns=Q_WIDTH,
    )
    up_came, passing, pairs, query_sent, output_kept = barrier(
        (up_came, passing, pairs, query_sent, output_kept)
    )

    query_came = swap_core(query_sent)
    output_came = chip_sends(output_kept)
    if unrolled:
        pair_one, pair_zero = pairs[0], pairs[1]
        passing = shift_z(add_low(add_low(own_one, pair_one), passing), -1)
    else:
        pair_zero = pairs
    passing, query_came, down_came, gate_came = barrier(
        (passing, query_came, down_came, gate_came)
    )

    query_kept = block_sums(query_kept, query_came)
    query_came = chip_sends(query_kept)
    gate_half = line_half(gate_sum, gate_came)
    gate_came = line_mid(gate_half)
    up_sum = chip_sum(up_kept, up_came)
    up_came = line_in(up_sum)
    down_total = line_total(down_half, down_came)
    down_came = line_out(down_total)
    last_kept, last_sent, d_rows = on_core(
        functools.partial(key_kernel, len(kv_pieces)),
        "key_value_grads",
        (
            (pieces_shape + (kv_pieces[0].shape[1],), BF16),
            (pieces_shape + (kv_pieces[0].shape[1],), BF16),
            ((model, token_rows), F32),
        ),
        places,
        own_zero,
        pair_zero,
        passing,
        cosine.T,
        sine.T,
        normed_one_turned,
        tokens_turned,
        inv_one.T,
        d_query_rows,
        grad_gain_two.T,
        *kv_pieces,
        estimate=cost(4 * token_rows * 2 * KV_WIDTH * model, 16 * token_rows * model),
        scratch=[pltpu.VMEM((token_rows, 2 * KV_WIDTH), BF16)],
        columns=kv_pieces[0].shape[1],
    )
    last_came = swap_core(last_sent)
    output_came, query_came, last_came, d_rows, gate_came, up_came = barrier(
        (output_came, query_came, last_came, d_rows, gate_came, up_came)
    )

    last_kept = block_sums(last_kept, last_came)
    last_came = chip_sends(last_kept)
    query_mine, query_came = x_parts(
        jnp.concatenate(
            [chip_sum(output_kept, output_came), chip_sum(query_kept, query_came)], 1
        )
    )
    query_came = swap_x(query_came)
    up_half = line_half(up_sum, up_came)
    up_came = line_mid(up_half)
    gate_total = line_total(gate_half, gate_came)
    gate_came = line_out(gate_total)
    last_came, query_came, up_came, down_came = barrier(
        (last_came, query_came, up_came, down_came)
    )

    last_mine, last_came = x_parts(chip_sum(last_kept, last_came))
    last_came = swap_x(last_came)
    query_sum = add_low(query_mine, query_came)
    query_came = line_in(query_sum)
    up_total = line_total(up_half, up_came)
    up_came = line_out(up_total)
    out_down = line_result(down_total, down_came).T.astype(F32)
    d_normed_one = d_rows.T
    scaled_one = d_normed_one * gain_one
    d_inputs = (
        d_hidden
        + inv_one * scaled_one
        - inputs * inv_one**3 * jnp.mean(scaled_one * inputs, -1, keepdims=True)
    )
    last_came, query_came, d_inputs, out_down = barrier(
        (last_came, query_came, d_inputs, out_down)
    )
    last_sum = add_low(last_mine, last_came)
    last_came = line_in(last_sum)
    query_half = line_half(query_sum, query_came)
    query_came = line_mid(query_half)
    feed_came = swap_x(feed_other)
    last_came, query_came, feed_came, up_came, gate_came = barrier(
        (last_came, query_came, feed_came, up_came, gate_came)
    )
    out_gate = line_result(gate_total, gate_came).astype(F32)
    out_up = line_result(up_total, up_came).astype(F32)

    last_half = line_half(last_sum, last_came)
    last_came = line_mid(last_half)
    query_total = line_total(query_half, query_came)
    query_came = line_out(query_total)
    result = (hidden_in + feed_own + feed_came.astype(F32)).astype(BF16)[None]
    last_came, query_came, result = barrier((last_came, query_came, result))

    last_total = line_total(last_half, last_came)
    last_came = line_out(last_total)
    query_mine = line_result(query_total, query_came)
    query_came = swap_x(query_mine)
    last_came, query_came, out_up, out_gate = barrier(
        (last_came, query_came, out_up, out_gate)
    )
    joined = x_join(query_mine, query_came)
    last_mine = line_result(last_total, last_came)
    last = x_join(last_mine, swap_x(last_mine))
    return (
        result,
        d_inputs[None],
        last[:, 2 * KV_WIDTH],
        last[:, 2 * KV_WIDTH + 1],
        joined[:, output_weight.shape[1] :],
        last[:, :KV_WIDTH],
        last[:, KV_WIDTH : 2 * KV_WIDTH],
        joined[:, : output_weight.shape[1]],
        out_gate,
        out_up,
        out_down,
    )


def solution(mesh):
    return jax.shard_map(
        shards,
        mesh=mesh,
        in_specs=(
            P("shard", ("ctx", "tensor"), None),
            P("shard", ("ctx", "tensor"), None),
            P("shard"),
            P("shard"),
            P("shard", None),
            P("shard", None),
            P("shard", None),
            P("shard", None),
            P("shard", "tensor"),
            P("shard", "tensor"),
            P("tensor", "shard"),
        ),
        out_specs=(
            P("shard", ("ctx", "tensor"), None),
            P("shard", ("ctx", "tensor"), None),
            P("shard"),
            P("shard"),
            P("shard", None),
            P("shard", None),
            P("shard", None),
            P("shard", None),
            P("shard", "tensor"),
            P("shard", "tensor"),
            P("tensor", "shard"),
        ),
        check_vma=False,
    )
```

```python
import functools

import jax
import jax.numpy as jnp
from jax import lax
from jax.experimental import pallas as pl
from jax.experimental.pallas import tpu as pltpu
from jax.sharding import PartitionSpec as P

QUERY_HEADS = 15
SHARED_KV_UNITS = 5
ATTN_UNIT_DIM = 64
GROUP = QUERY_HEADS // SHARED_KV_UNITS
KV_WIDTH = SHARED_KV_UNITS * ATTN_UNIT_DIM
Q_WIDTH = QUERY_HEADS * ATTN_UNIT_DIM

EPS = 1e-05
THETA = 100000.0
F32 = jnp.float32
BF16 = jnp.bfloat16
barrier = lax.optimization_barrier


def rotary_tables(positions):
    half = ATTN_UNIT_DIM // 2
    freqs = THETA ** (-(jnp.arange(half, dtype=F32) * 2.0 / ATTN_UNIT_DIM))
    angles = freqs[:, None] * positions.astype(F32)[None, :]
    return (jnp.cos(angles), jnp.sin(angles))


def rotate(block, cosine, sine):
    split = block.reshape(-1, 2, ATTN_UNIT_DIM // 2, block.shape[1])
    former, latter = split[:, 0], split[:, 1]
    turned = jnp.stack([former * cosine - latter * sine, latter * cosine + former * sine], 1)
    return turned.reshape(block.shape)


def rotate_lanes(block, cosine, sine):
    split = block.reshape(block.shape[0], -1, 2, ATTN_UNIT_DIM // 2)
    former, latter = split[:, :, 0], split[:, :, 1]
    cosine, sine = cosine[:, None, :], sine[:, None, :]
    turned = jnp.stack([former * cosine - latter * sine, latter * cosine + former * sine], 2)
    return turned.reshape(block.shape)


def product(left, right, left_dim, right_dim):
    return lax.dot_general(
        left, right, (((left_dim,), (right_dim,)), ((), ())), preferred_element_type=F32
    )


def swap_core(block):
    size = lax.axis_size("shard")
    return lax.ppermute(block, "shard", [(i, i ^ 1) for i in range(size)])


def shift_y(block, step):
    size = lax.axis_size("shard")
    return lax.ppermute(block, "shard", [(i, (i + 2 * step) % size) for i in range(size)])


def swap_x(block):
    return lax.ppermute(block, "tensor", [(0, 1), (1, 0)])


def shift_z(block, step):
    size = lax.axis_size("ctx")
    pairs = [(i, i + step) for i in range(size) if 0 <= i + step < size]
    return lax.ppermute(block, "ctx", pairs)


def from_other_chips(own):
    return [shift_y(own, -step) for step in range(1, lax.axis_size("shard") // 2)]


def both_cores(held):
    return [piece for block in held for piece in (block, swap_core(block))]


def near_places():
    size = lax.axis_size("shard")
    me = lax.axis_index("shard")
    places = []
    for step in range(size // 2):
        owner = lax.rem(me + 2 * step, size)
        places += [owner, jnp.bitwise_xor(owner, 1)]
    return places


def near_pieces(whole, dim):
    width = whole.shape[dim] // lax.axis_size("shard")
    return [lax.dynamic_slice_in_dim(whole, p * width, width, dim) for p in near_places()]


def in_order(pieces, dim):
    places = near_places()
    ordered = []
    for index in range(len(pieces)):
        piece = pieces[0]
        for place, other in zip(places[1:], pieces[1:]):
            piece = jnp.where(place == index, other, piece)
        ordered.append(piece)
    return jnp.concatenate(ordered, dim)


def add_low(left, right):
    return (left.astype(F32) + right.astype(F32)).astype(BF16)


def block_sums(kept, came):
    return [add_low(kept[step], came[step]) for step in range(kept.shape[0])]


def chip_sends(kept):
    return [shift_y(block, step) for step, block in enumerate(kept) if step > 0]


def chip_sum(kept, came):
    total = kept[0].astype(F32)
    for block in came:
        total = total + block.astype(F32)
    return total.astype(BF16)


def on_line():
    return lax.axis_size("ctx") == 4


def line_in(block):
    return lax.ppermute(block, "ctx", [(0, 1), (3, 2)]) if on_line() else block


def line_mid(half):
    return lax.ppermute(half, "ctx", [(1, 2), (2, 1)]) if on_line() else half


def line_out(total):
    return lax.ppermute(total, "ctx", [(1, 0), (2, 3)]) if on_line() else total


def line_half(block, came):
    return add_low(block, came) if on_line() else lax.psum(block, "ctx")


def line_total(half, came):
    return add_low(half, came) if on_line() else half


def line_result(total, came):
    if not on_line():
        return total
    me = lax.axis_index("ctx")
    return jnp.where(jnp.logical_or(me == 1, me == 2), total, came)


def x_parts(block):
    half = block.shape[0] // 2
    me = lax.axis_index("tensor")
    kept = lax.dynamic_slice_in_dim(block, me * half, half, 0)
    sent = lax.dynamic_slice_in_dim(block, (1 - me) * half, half, 0)
    return kept, sent


def x_join(block, other):
    first = lax.axis_index("tensor") == 0
    return jnp.concatenate(
        [jnp.where(first, block, other), jnp.where(first, other, block)], 0
    ).astype(F32)


def head_part(head, offset=0):
    return slice(offset + head * ATTN_UNIT_DIM, offset + (head + 1) * ATTN_UNIT_DIM)


def causal_mask(keys, lanes, rows):
    key = lax.broadcasted_iota(jnp.int32, (keys, lanes), 0)
    lane = lax.broadcasted_iota(jnp.int32, (keys, lanes), 1)
    return key <= lax.rem(lane, rows)


def forward_first_kernel(query_ref, tile_ref, stats_ref, accum_ref):
    rows = tile_ref.shape[0]
    lanes = query_ref.shape[1]
    mask = causal_mask(rows, lanes, rows)
    stats_ref[...] = jnp.zeros_like(stats_ref)
    for head in range(SHARED_KV_UNITS):
        key = tile_ref[:, head_part(head)]
        value = tile_ref[:, head_part(head, KV_WIDTH)]
        scores = jnp.dot(key, query_ref[head_part(head), :], preferred_element_type=F32)
        scores = jnp.where(mask, scores, -1e30)
        peak = jnp.max(scores, 0, keepdims=True)
        probs = jnp.exp(scores - peak)
        stats_ref[head : head + 1, :] = peak
        stats_ref[8 + head : 9 + head, :] = jnp.sum(probs, 0, keepdims=True)
        accum_ref[head_part(head), :] = product(value, probs.astype(BF16), 0, 0)


def forward_kernel(count, flags_ref, query_ref, *refs):
    tiles, (stats_in, accum_in, stats_ref, accum_ref) = refs[:count], refs[count:]
    stats_ref[...] = stats_in[...]
    accum_ref[...] = accum_in[...]
    for index, tile_ref in enumerate(tiles):

        @pl.when(flags_ref[index] != 0)
        def _(tile_ref=tile_ref):
            for head in range(SHARED_KV_UNITS):
                key = tile_ref[:, head_part(head)]
                value = tile_ref[:, head_part(head, KV_WIDTH)]
                scores = jnp.dot(key, query_ref[head_part(head), :], preferred_element_type=F32)
                old_peak = stats_ref[head : head + 1, :]
                peak = jnp.maximum(old_peak, jnp.max(scores, 0, keepdims=True))
                probs = jnp.exp(scores - peak)
                rescale = jnp.exp(old_peak - peak)
                total = stats_ref[8 + head : 9 + head, :]
                stats_ref[head : head + 1, :] = peak
                stats_ref[8 + head : 9 + head, :] = total * rescale + jnp.sum(
                    probs, 0, keepdims=True
                )
                accum_ref[head_part(head), :] = accum_ref[head_part(head), :] * rescale + (
                    product(value, probs.astype(BF16), 0, 0)
                )


def backward_kernel(causal, count, flags_ref, query_ref, grad_ref, stats_ref, *refs):
    tiles, (into, out_ref), sums = refs[:count], refs[count : count + 2], refs[count + 2 :]
    if len(sums) < count:
        sums = (sums[0], sums[1].at[0], sums[1].at[1])
    rows = tiles[0].shape[0]
    lanes = query_ref.shape[1]
    out_ref[...] = into[...]
    for index, (tile_ref, sum_ref) in enumerate(zip(tiles, sums)):

        @pl.when(flags_ref[index] == 0)
        def _(sum_ref=sum_ref):
            sum_ref[...] = jnp.zeros_like(sum_ref)

        @pl.when(flags_ref[index] != 0)
        def _(tile_ref=tile_ref, sum_ref=sum_ref):
            for head in range(SHARED_KV_UNITS):
                key = tile_ref[:, head_part(head)]
                value = tile_ref[:, head_part(head, KV_WIDTH)]
                query = query_ref[head_part(head), :]
                grad = grad_ref[head_part(head), :]
                scores = jnp.dot(key, query, preferred_element_type=F32)
                probs = jnp.exp(scores - stats_ref[head : head + 1, :])
                if causal:
                    probs = jnp.where(causal_mask(rows, lanes, rows), probs, 0.0)
                d_probs = jnp.dot(value, grad, preferred_element_type=F32)
                d_scores = (probs * (d_probs - stats_ref[8 + head : 9 + head, :])).astype(BF16)
                sum_ref[:, head_part(head)] = product(d_scores, query, 1, 1).astype(BF16)
                sum_ref[:, head_part(head, KV_WIDTH)] = product(
                    probs.astype(BF16), grad, 1, 1
                ).astype(BF16)
                out_ref[head_part(head), :] += product(key, d_scores, 0, 0)


def cost(multiply_adds, values=0, transcendentals=0):
    return pl.CostEstimate(
        flops=2 * multiply_adds, bytes_accessed=values, transcendentals=transcendentals
    )


def tile_cost(count, rows, lanes, matmuls):
    return cost(
        4 * matmuls * count * rows * lanes * KV_WIDTH,
        8 * KV_WIDTH * lanes,
        count * rows * lanes * SHARED_KV_UNITS,
    )


MEMORY = pltpu.CompilerParams(vmem_limit_bytes=24 * 1024 * 1024)
LARGE = pltpu.CompilerParams(vmem_limit_bytes=58 * 1024 * 1024)
IN_VMEM = pl.BlockSpec(memory_space=pltpu.VMEM)
IN_SMEM = pl.BlockSpec(memory_space=pltpu.SMEM)


def on_core(
    kernel, name, out_shape, *operands, estimate, scratch=(), first_in_smem=True, columns=None
):
    def block(shape):
        return pl.BlockSpec(shape, lambda i: (0,) * len(shape))

    specs = [IN_VMEM] * len(operands)
    outs = [IN_VMEM] * len(out_shape)
    if columns is not None:
        last = operands[-1].shape
        specs = [
            block((last[0], columns) if operand.shape == last else operand.shape)
            for operand in operands
        ]
        outs = [block(shape[0]) for shape in out_shape]
    if first_in_smem:
        specs[0] = IN_SMEM
    return pl.pallas_call(
        kernel,
        grid=() if columns is None else (1,),
        in_specs=specs,
        out_specs=tuple(outs),
        out_shape=tuple(jax.ShapeDtypeStruct(*shape) for shape in out_shape),
        scratch_shapes=list(scratch),
        cost_estimate=estimate,
        compiler_params=MEMORY if columns is None else LARGE,
        name=name,
    )(*operands)


def forward_first(query, tile):
    lanes = query.shape[1]
    return on_core(
        forward_first_kernel,
        "attend_own",
        (((16, lanes), F32), ((KV_WIDTH, lanes), F32)),
        query,
        tile,
        estimate=tile_cost(1, tile.shape[0], lanes, 2),
        first_in_smem=False,
    )


def forward_tiles(query, tiles, flags, stats, accum):
    return on_core(
        functools.partial(forward_kernel, len(tiles)),
        "attend",
        ((stats.shape, F32), (accum.shape, F32)),
        jnp.stack(flags).astype(jnp.int32),
        query,
        *tiles,
        stats,
        accum,
        estimate=tile_cost(len(tiles), tiles[0].shape[0], query.shape[1], 2),
    )


def backward_tiles(query, grad, stats, tiles, flags, into, causal=False):
    shape = tiles[0].shape
    sums = (shape, (2,) + shape) if len(tiles) == 3 else (shape,) * len(tiles)
    out = on_core(
        functools.partial(backward_kernel, causal, len(tiles)),
        "attend_back",
        ((into.shape, F32),) + tuple((item, BF16) for item in sums),
        jnp.stack(flags).astype(jnp.int32),
        query,
        grad,
        stats,
        *tiles,
        into,
        estimate=tile_cost(len(tiles), tiles[0].shape[0], query.shape[1], 20),
    )
    return out[0], out[1:]


def to_lanes(block):
    rows = block.shape[1]
    split = block.reshape(SHARED_KV_UNITS, GROUP, ATTN_UNIT_DIM, rows)
    return split.transpose(0, 2, 1, 3).reshape(KV_WIDTH, GROUP * rows)


def place_rows(places, index, width):
    return pl.ds(pl.multiple_of(places[index] * width, 16), width)


def put_in_order(places, pieces, whole, columns):
    width = pieces[0].shape[0]
    for index, piece in enumerate(pieces):
        whole[place_rows(places, index, width), :] = piece[:, :columns]


def mid_kernel(count, places, stats, accum, inputs, gain, *refs):
    weights = refs[:count]
    attended_ref, hidden_ref, normed_ref, weight = refs[count:]
    rows, model = inputs.shape
    put_in_order(places, weights, weight, model)
    for head in range(SHARED_KV_UNITS):
        part = accum[head_part(head), :] / stats[8 + head : 9 + head, :]
        for member in range(GROUP):
            attended_ref[head_part(head * GROUP + member), :] = part[
                :, member * rows : (member + 1) * rows
            ].astype(BF16)
    hidden = inputs[...].astype(F32) + product(attended_ref[...], weight[...], 0, 0)
    hidden_ref[...] = hidden
    inverse = lax.rsqrt(jnp.mean(hidden * hidden, -1, keepdims=True) + EPS)
    normed_ref[:, :model] = (hidden * inverse * gain[...]).astype(BF16)
    normed_ref[:, model:] = jnp.zeros((rows, normed_ref.shape[1] - model), BF16)


def feed_kernel(count, places, *refs):
    normed_own, normed_other, upstream_own, upstream_other = refs[:4]
    gates, ups, downs = (refs[4 + k * count : 4 + (k + 1) * count] for k in range(3))
    units_ref, turned, feed_own, feed_other, grad_own, grad_other = refs[
        4 + 3 * count : 10 + 3 * count
    ]
    gate, up, down, normed, upstream, feed_sum, grad_sum = refs[10 + 3 * count :]
    rows = normed_own.shape[0]
    model, tile = gate.shape

    @pl.when(pl.program_id(0) == 0)
    def _():
        normed[:rows, :] = normed_own[...]
        normed[rows:, :] = normed_other[...]
        turned[...] = normed[...].T
        upstream[:rows, :] = upstream_own[...]
        upstream[rows:, :] = upstream_other[...]
        feed_sum[...] = jnp.zeros_like(feed_sum)
        grad_sum[...] = jnp.zeros_like(grad_sum)

    for pieces, whole in ((gates, gate), (ups, up), (downs, down)):
        put_in_order(places, pieces, whole, tile)
    gate_val = jnp.dot(normed[:, :model], gate[...], preferred_element_type=F32)
    up_val = jnp.dot(normed[:, :model], up[...], preferred_element_type=F32)
    d_product = jnp.dot(upstream[...], down[...], preferred_element_type=F32)
    sigmoid = 0.5 * jnp.tanh(0.5 * gate_val) + 0.5
    silu = gate_val * sigmoid
    z = (silu * up_val).astype(BF16)
    d_up = (d_product * silu).astype(BF16)
    d_gate = (d_product * up_val * sigmoid * (1.0 + gate_val * (1.0 - sigmoid))).astype(BF16)
    units_ref[:, :tile] = z
    units_ref[:, tile : 2 * tile] = d_gate
    units_ref[:, 2 * tile :] = d_up
    grad_sum[...] += product(d_gate, gate[...], 1, 1) + product(d_up, up[...], 1, 1)
    feed_sum[...] += product(z, down[...], 1, 1)

    @pl.when(pl.program_id(0) == pl.num_programs(0) - 1)
    def _():
        for total, own, other in ((feed_sum, feed_own, feed_other), (grad_sum, grad_own, grad_other)):
            own[...] = total[:rows, :]
            other[...] = total[rows:, :].astype(BF16)


def feed_tile(units):
    return units // 2


def feed_forward(places, rows_in, packed, units):
    count = len(packed)
    rows, wide = rows_in[0].shape
    model = rows_in[2].shape[1]
    width = packed[0].shape[0]
    tile = feed_tile(units)
    steps = units // tile
    whole = pl.BlockSpec((rows, model), lambda i: (0, 0))
    wide_spec = pl.BlockSpec((rows, wide), lambda i: (0, 0))
    gate_spec = pl.BlockSpec((width, tile), lambda i: (0, i))
    up_spec = pl.BlockSpec((width, tile), lambda i: (0, i + steps))
    down_spec = pl.BlockSpec((width, tile), lambda i: (0, i + 2 * steps))
    out_spec = pl.BlockSpec((2 * rows, 3 * tile), lambda i: (0, i))
    return pl.pallas_call(
        functools.partial(feed_kernel, count),
        grid=(steps,),
        in_specs=[IN_SMEM, wide_spec, wide_spec, whole, whole]
        + [gate_spec] * count
        + [up_spec] * count
        + [down_spec] * count,
        out_specs=(out_spec, pl.BlockSpec((wide, 2 * rows), lambda i: (0, 0))) + (whole,) * 4,
        out_shape=(
            jax.ShapeDtypeStruct((2 * rows, 3 * units), BF16),
            jax.ShapeDtypeStruct((wide, 2 * rows), BF16),
        )
        + (
            jax.ShapeDtypeStruct((rows, model), F32),
            jax.ShapeDtypeStruct((rows, model), BF16),
        )
        * 2,
        scratch_shapes=[pltpu.VMEM((model, tile), BF16)] * 3
        + [pltpu.VMEM((2 * rows, wide), BF16), pltpu.VMEM((2 * rows, model), BF16)]
        + [pltpu.VMEM((2 * rows, model), F32)] * 2,
        cost_estimate=cost(12 * rows * model * units, 6 * model * units, rows * units),
        compiler_params=LARGE,
        name="feed_forward",
    )(places, *rows_in, *packed, *packed, *packed)


def grad_kernel(count, width, places, turned, values, kept, sent):
    for index in range(count):
        total = jnp.dot(
            turned[place_rows(places, index, width), :], values[...], preferred_element_type=F32
        )
        (kept, sent)[index % 2][index // 2] = total.astype(BF16)


def feed_grads(places, turned, values, units, model, which):
    count = lax.axis_size("shard")
    rows = turned.shape[1]
    width = model // count
    tile = feed_tile(units)
    whole = pl.BlockSpec(turned.shape, lambda i: (0, 0))
    sum_spec = pl.BlockSpec((count // 2, width, tile), lambda i: (0, 0, i))
    return pl.pallas_call(
        functools.partial(grad_kernel, count, width),
        grid=(units // tile,),
        in_specs=[IN_SMEM, whole, pl.BlockSpec((rows, tile), lambda i: (0, 3 * i + which))],
        out_specs=(sum_spec,) * 2,
        out_shape=(jax.ShapeDtypeStruct((count // 2, width, units), BF16),) * 2,
        cost_estimate=cost(2 * rows * model * units, 4 * model * units),
        compiler_params=LARGE,
        name="feed_grads",
    )(places, turned, values)


def turn_kernel(count, places, *refs):
    own, came, hidden_ref, upstream, gain, attended, accum, stats = refs[:8]
    weights = refs[8 : 8 + count]
    d_hidden_ref, grads, stats_ref, kept, sent, gain_ref, turned = refs[8 + count :]
    rows, model = hidden_ref.shape
    width = weights[0].shape[0]
    hidden = hidden_ref[...]
    d_normed = own[...] + came[...].astype(F32)
    inverse = lax.rsqrt(jnp.mean(hidden * hidden, -1, keepdims=True) + EPS)
    gain_ref[...] = jnp.sum(d_normed * hidden * inverse, 0, keepdims=True)
    scaled = d_normed * gain[...]
    d_hidden = (
        upstream[...].astype(F32)
        + inverse * scaled
        - hidden * (inverse * inverse * inverse * jnp.mean(scaled * hidden, -1, keepdims=True))
    )
    d_hidden_ref[...] = d_hidden
    d_branch = d_hidden.astype(BF16)
    for index, weight in enumerate(weights):
        part = place_rows(places, index, width)
        turned[part, :] = product(weight[:, :model], d_branch, 1, 1).astype(BF16)
        (kept, sent)[index % 2][index // 2] = jnp.dot(
            attended[part, :], d_branch, preferred_element_type=F32
        ).astype(BF16)
    stats_ref[...] = jnp.zeros_like(stats_ref)
    for head in range(SHARED_KV_UNITS):
        for member in range(GROUP):
            lanes = slice(member * rows, (member + 1) * rows)
            grads[head_part(head), lanes] = turned[head_part(head * GROUP + member), :]
        total = stats[8 + head : 9 + head, :]
        stats_ref[head : head + 1, :] = stats[head : head + 1, :] + jnp.log(total)
        stats_ref[8 + head : 9 + head, :] = jnp.sum(
            grads[head_part(head), :].astype(F32) * (accum[head_part(head), :] / total),
            0,
            keepdims=True,
        )


def query_kernel(count, places, d_query, cosine, sine, normed, *refs):
    weights = refs[:count]
    kept, sent, d_rows, turned = refs[count:]
    rows = normed.shape[1]
    width = weights[0].shape[0]
    half = ATTN_UNIT_DIM // 2
    scale = ATTN_UNIT_DIM ** (-0.5)
    for head in range(SHARED_KV_UNITS):
        for member in range(GROUP):
            lanes = slice(member * rows, (member + 1) * rows)
            start = head * ATTN_UNIT_DIM
            former = d_query[start : start + half, lanes] * scale
            latter = d_query[start + half : start + 2 * half, lanes] * scale
            start = (head * GROUP + member) * ATTN_UNIT_DIM
            turned[start : start + half, :] = (
                former * cosine[...] + latter * sine[...]
            ).astype(BF16)
            turned[start + half : start + 2 * half, :] = (
                latter * cosine[...] - former * sine[...]
            ).astype(BF16)
    for index, weight in enumerate(weights):
        part = place_rows(places, index, width)
        (kept, sent)[index % 2][index // 2] = product(normed[part, :], turned[...], 1, 1).astype(
            BF16
        )
        d_rows[part, :] = jnp.dot(weight[...], turned[...], preferred_element_type=F32)


def key_kernel(count, places, *refs):
    own, pair, passing, cosine, sine, normed, inputs, inverse, d_query_rows, gain = refs[:10]
    weights = refs[10 : 10 + count]
    kept, sent, d_rows, turned = refs[10 + count :]
    width = normed.shape[0] // count
    half = ATTN_UNIT_DIM // 2
    total = own[...].astype(F32) + pair[...].astype(F32) + passing[...].astype(F32)
    for head in range(SHARED_KV_UNITS):
        start = head * ATTN_UNIT_DIM
        former = total[:, start : start + half]
        latter = total[:, start + half : start + 2 * half]
        turned[:, start : start + half] = (former * cosine[...] + latter * sine[...]).astype(BF16)
        turned[:, start + half : start + 2 * half] = (
            latter * cosine[...] - former * sine[...]
        ).astype(BF16)
    turned[:, KV_WIDTH:] = total[:, KV_WIDTH:].astype(BF16)
    for index, weight in enumerate(weights):
        part = place_rows(places, index, width)
        d_part = d_query_rows[part, :] + product(weight[:width, :], turned[...], 1, 1)
        d_rows[part, :] = d_part
        own_gain = jnp.sum(
            d_part * inputs[part, :].astype(F32) * inverse[...], 1, keepdims=True
        )
        target = (kept, sent)[index % 2]
        target[index // 2, :, : 2 * KV_WIDTH] = jnp.dot(
            normed[part, :], turned[...], preferred_element_type=F32
        ).astype(BF16)
        side = target.shape[2] - 2 * KV_WIDTH
        lane = lax.broadcasted_iota(jnp.int32, (width, side), 1)
        target[index // 2, :, 2 * KV_WIDTH :] = jnp.where(
            lane == 0, own_gain, jnp.where(lane == 1, gain[part, :], 0.0)
        ).astype(BF16)


def shards(
    tokens,
    cotangent,
    prenorm_scaling,
    hidden_gain,
    query_weight,
    key_matrix,
    value_matrix,
    output_weight,
    gate_weight,
    up_weight,
    down_weight,
):
    token_rows = tokens.shape[1]
    units = gate_weight.shape[1]
    ctx_size = lax.axis_size("ctx")
    ctx_me = lax.axis_index("ctx")
    tensor_me = lax.axis_index("tensor")
    scale_factor = ATTN_UNIT_DIM ** (-0.5)
    positions = (ctx_me * 2 + tensor_me) * token_rows + jnp.arange(token_rows, dtype=jnp.int32)
    cosine, sine = rotary_tables(positions)
    inputs = tokens[0].astype(F32)
    unrolled = ctx_size == 4

    gains = jnp.stack([prenorm_scaling, hidden_gain]).astype(BF16)
    own_rows = key_matrix.shape[0]
    own_kv = jnp.concatenate(
        [
            jnp.concatenate([key_matrix, value_matrix], 1),
            jnp.pad(gains, ((0, 14), (0, 2 * KV_WIDTH - own_rows))),
        ],
        0,
    )
    far_kv = from_other_chips(own_kv)
    other_cotangent = swap_x(cotangent[0])
    inv_one = lax.rsqrt(jnp.mean(inputs * inputs, -1, keepdims=True) + EPS)
    far_kv, query_weight, inv_one, tokens_turned = barrier(
        (far_kv, query_weight, inv_one, tokens[0].T)
    )
    far_query = from_other_chips(query_weight)
    kv_pieces = both_cores([own_kv] + far_kv)
    gains = in_order(
        [piece[own_rows : own_rows + 2, :own_rows] for piece in kv_pieces], 1
    ).astype(F32)
    gain_one, gain_two = gains[0], gains[1]
    places = jnp.stack(near_places()).astype(jnp.int32)

    normed_one = (inputs * inv_one * gain_one).astype(BF16)
    normed_one_turned = normed_one.T
    near_one = near_pieces(normed_one, 1)
    projected = sum(
        product(rows, weight[:own_rows], 1, 0) for weight, rows in zip(kv_pieces, near_one)
    )
    key_value = jnp.concatenate(
        [
            rotate_lanes(projected[:, :KV_WIDTH], cosine.T, sine.T).astype(BF16),
            projected[:, KV_WIDTH:].astype(BF16),
        ],
        1,
    )
    far_query, output_weight, other_cotangent, gate_weight = barrier(
        (far_query, output_weight, other_cotangent, gate_weight)
    )
    turned_upstream = jnp.concatenate([cotangent[0], other_cotangent], 0).T
    own_ffn = jnp.concatenate([gate_weight, up_weight, down_weight.T], 1)
    far_output = from_other_chips(output_weight)
    query_pieces = both_cores([query_weight] + far_query)
    query_projected = sum(
        product(weight, rows, 0, 1) for weight, rows in zip(query_pieces, near_one)
    )
    queries = to_lanes((rotate(query_projected, cosine, sine) * scale_factor).astype(BF16))
    later = tensor_me == 1
    flags = [(later if step == 0 else ctx_me >= step) for step in range(ctx_size)]
    passing = key_value
    passing = shift_z(key_value, 1)
    pair_zero = swap_x(key_value)
    stats, accum = forward_first(queries, key_value)
    pair_one, after = swap_x(passing), shift_z(passing, 1)
    stats, accum = forward_tiles(queries, [pair_zero], [flags[0]], stats, accum)
    far_output, own_ffn, stats, pair_one, after = barrier(
        (far_output, own_ffn, stats, pair_one, after)
    )
    far_ffn = from_other_chips(own_ffn)
    tiles = [(key_value, pair_zero), (passing, pair_one), (after, swap_x(after))]
    if unrolled:
        stats, accum = forward_tiles(queries, tiles[1], [flags[1]] * 2, stats, accum)
        after, stats = barrier((shift_z(after, 1), stats))
        tiles.append((after, swap_x(after)))
    for step in range(3, 3 if unrolled else ctx_size):
        after = shift_z(after, 1)
        tiles.append((after, swap_x(after)))
    if unrolled:
        for step in range(2, ctx_size):
            stats, accum = forward_tiles(queries, tiles[step], [flags[step]] * 2, stats, accum)
    else:
        scanned = (
            jnp.stack([tile[0] for tile in tiles[1:]]),
            jnp.stack([tile[1] for tile in tiles[1:]]),
            jnp.stack(flags[1:]),
        )
        (stats, accum), unused = lax.scan(
            lambda held, item: (
                forward_tiles(queries, [item[0], item[1]], [item[2], item[2]], *held),
                None,
            ),
            (stats, accum),
            scanned,
        )

    output_pieces = both_cores([output_weight] + far_output)
    model = tokens.shape[2]
    wide = -(-model // 128) * 128
    attended, hidden_in, normed_two = on_core(
        functools.partial(mid_kernel, len(output_pieces)),
        "attended_to_normed",
        (
            ((Q_WIDTH, token_rows), BF16),
            ((token_rows, model), F32),
            ((token_rows, wide), BF16),
        ),
        places,
        stats,
        accum,
        tokens[0],
        gain_two[None],
        *output_pieces,
        estimate=cost(2 * token_rows * Q_WIDTH * model, 8 * token_rows * model),
        scratch=[pltpu.VMEM((Q_WIDTH, model), BF16)],
        columns=model,
    )
    near_ffn = swap_core(own_ffn)
    normed_two, far_ffn, near_ffn = barrier((normed_two, far_ffn, near_ffn))
    other_normed = swap_x(normed_two)
    ffn_pieces = [own_ffn, near_ffn] + both_cores(far_ffn)
    unit_values, turned, feed_own, feed_other, d_normed_own, d_normed_other = feed_forward(
        places,
        [normed_two, other_normed, cotangent[0], other_cotangent],
        ffn_pieces,
        units,
    )

    d_normed_came = swap_x(d_normed_other)
    kept_down, down_sent = feed_grads(places, turned_upstream, unit_values, units, model, 0)
    kept_gate, gate_sent = feed_grads(places, turned, unit_values, units, model, 1)
    kept_up, up_sent = feed_grads(places, turned, unit_values, units, model, 2)
    down_came = swap_core(down_sent)
    gate_came = swap_core(gate_sent)
    up_came = swap_core(up_sent)

    lanes = queries.shape[1]
    pieces_shape = (len(output_pieces) // 2, query_weight.shape[0])
    d_hidden, grads, stats, output_kept, output_sent, grad_gain_two = on_core(
        functools.partial(turn_kernel, len(output_pieces)),
        "normed_to_attended",
        (
            ((token_rows, model), F32),
            ((KV_WIDTH, lanes), BF16),
            ((16, lanes), F32),
            (pieces_shape + (model,), BF16),
            (pieces_shape + (model,), BF16),
            ((1, model), F32),
        ),
        places,
        d_normed_own,
        d_normed_came,
        hidden_in,
        cotangent[0],
        gain_two[None],
        attended,
        accum,
        stats,
        *output_pieces,
        estimate=cost(40 * token_rows * Q_WIDTH * model, 16 * token_rows * model),
        scratch=[pltpu.VMEM((Q_WIDTH, token_rows), BF16)],
        columns=model,
    )
    output_sent, down_came, gate_came, d_query = barrier(
        (output_sent, down_came, gate_came, jnp.zeros(accum.shape, F32))
    )
    down_kept = block_sums(kept_down, down_came)
    down_came = chip_sends(down_kept)
    gate_kept = block_sums(kept_gate, gate_came)
    gate_came = chip_sends(gate_kept)

    output_came = swap_core(output_sent)
    d_parts = {}
    if unrolled:
        d_query, d_parts[3] = backward_tiles(
            queries, grads, stats, tiles[3], [flags[3]] * 2, d_query
        )
        pair_three = swap_x(d_parts[3][1])
    else:
        d_query, terms = lax.scan(
            lambda held, item: backward_tiles(
                queries, grads, stats, [item[0], item[1]], [item[2], item[2]], held
            ),
            d_query,
            scanned,
        )
        passing = None
        for step in reversed(range(1, ctx_size)):
            part = add_low(terms[0][step - 1], swap_x(terms[1][step - 1]))
            part = part if passing is None else add_low(part, passing)
            passing = shift_z(part, -1)
        pair_three = passing
    down_came, d_query = barrier((down_came, d_query))
    down_sum = chip_sum(down_kept, down_came)
    down_came = line_in(down_sum)
    if unrolled:
        d_query, d_parts[2] = backward_tiles(
            queries, grads, stats, tiles[2], [flags[2]] * 2, d_query
        )
    up_came, output_came, pair_three, d_query = barrier(
        (up_came, output_came, pair_three, d_query)
    )

    up_kept = block_sums(kept_up, up_came)
    up_came = chip_sends(up_kept)
    output_kept = block_sums(output_kept, output_came)
    passing = pair_three
    pair_two = pair_three
    if unrolled:
        pair_two = swap_x(d_parts[2][1])
        passing = shift_z(add_low(d_parts[3][0], pair_three), -1)
        d_query, (own_one, pairs) = backward_tiles(
            queries,
            grads,
            stats,
            [tiles[1][0], tiles[1][1], tiles[0][1]],
            [flags[1], flags[1], flags[0]],
            d_query,
        )
        pair_two, passing, gate_came, down_came, d_query = barrier(
            (pair_two, passing, gate_came, down_came, d_query)
        )
        passing = shift_z(add_low(add_low(d_parts[2][0], pair_two), passing), -1)
    else:
        d_query, (pairs,) = backward_tiles(
            queries, grads, stats, [tiles[0][1]], [flags[0]], d_query
        )
    d_query, (own_zero,) = backward_tiles(
        queries, grads, stats, [key_value], [ctx_me >= 0], d_query, causal=True
    )
    gate_sum = chip_sum(gate_kept, gate_came)
    gate_came = line_in(gate_sum)
    down_half = line_half(down_sum, down_came)
    down_came = line_mid(down_half)
    pairs = swap_x(pairs)
    query_kept, query_sent, d_query_rows = on_core(
        functools.partial(query_kernel, len(query_pieces)),
        "query_grads",
        (
            (pieces_shape + (Q_WIDTH,), BF16),
            (pieces_shape + (Q_WIDTH,), BF16),
            ((model, token_rows), F32),
        ),
        places,
        d_query,
        cosine,
        sine,
        normed_one_turned,
        *query_pieces,
        estimate=cost(4 * token_rows * Q_WIDTH * model, 16 * token_rows * model),
        scratch=[pltpu.VMEM((Q_WIDTH, token_rows), BF16)],
        columns=Q_WIDTH,
    )
    up_came, passing, pairs, query_sent, output_kept = barrier(
        (up_came, passing, pairs, query_sent, output_kept)
    )

    query_came = swap_core(query_sent)
    if unrolled:
        pair_one, pair_zero = pairs[0], pairs[1]
        passing = shift_z(add_low(add_low(own_one, pair_one), passing), -1)
    else:
        pair_zero = pairs
    passing, query_came, down_came, gate_came, d_hidden, grad_gain_two = barrier(
        (passing, query_came, down_came, gate_came, d_hidden, grad_gain_two)
    )

    query_kept = [
        jnp.concatenate([output, query], 1)
        for output, query in zip(output_kept, block_sums(query_kept, query_came))
    ]
    query_came = chip_sends(query_kept)
    gate_half = line_half(gate_sum, gate_came)
    gate_came = line_mid(gate_half)
    up_sum = chip_sum(up_kept, up_came)
    up_came = line_in(up_sum)
    down_total = line_total(down_half, down_came)
    down_came = line_out(down_total)
    last_kept, last_sent, d_rows = on_core(
        functools.partial(key_kernel, len(kv_pieces)),
        "key_value_grads",
        (
            (pieces_shape + (2 * KV_WIDTH + 128,), BF16),
            (pieces_shape + (2 * KV_WIDTH + 128,), BF16),
            ((model, token_rows), F32),
        ),
        places,
        own_zero,
        pair_zero,
        passing,
        cosine.T,
        sine.T,
        normed_one_turned,
        tokens_turned,
        inv_one.T,
        d_query_rows,
        grad_gain_two.T,
        *kv_pieces,
        estimate=cost(4 * token_rows * 2 * KV_WIDTH * model, 16 * token_rows * model),
        scratch=[pltpu.VMEM((token_rows, 2 * KV_WIDTH), BF16)],
        columns=kv_pieces[0].shape[1],
    )
    last_came = swap_core(last_sent)
    query_came, last_came, d_rows, gate_came, up_came = barrier(
        (query_came, last_came, d_rows, gate_came, up_came)
    )

    last_kept = block_sums(last_kept, last_came)
    last_came = chip_sends(last_kept)
    query_mine, query_came = x_parts(chip_sum(query_kept, query_came))
    query_came = swap_x(query_came)
    up_half = line_half(up_sum, up_came)
    up_came = line_mid(up_half)
    gate_total = line_total(gate_half, gate_came)
    gate_came = line_out(gate_total)
    last_came, query_came, up_came, down_came = barrier(
        (last_came, query_came, up_came, down_came)
    )

    last_mine, last_came = x_parts(chip_sum(last_kept, last_came))
    last_came = swap_x(last_came)
    query_sum = add_low(query_mine, query_came)
    query_came = line_in(query_sum)
    up_total = line_total(up_half, up_came)
    up_came = line_out(up_total)
    out_down = line_result(down_total, down_came).T.astype(F32)
    d_normed_one = d_rows.T
    scaled_one = d_normed_one * gain_one
    d_inputs = (
        d_hidden
        + inv_one * scaled_one
        - inputs * inv_one**3 * jnp.mean(scaled_one * inputs, -1, keepdims=True)
    )
    last_came, query_came, d_inputs, out_down = barrier(
        (last_came, query_came, d_inputs, out_down)
    )
    last_sum = add_low(last_mine, last_came)
    last_came = line_in(last_sum)
    query_half = line_half(query_sum, query_came)
    query_came = line_mid(query_half)
    feed_came = swap_x(feed_other)
    last_came, query_came, feed_came, up_came, gate_came = barrier(
        (last_came, query_came, feed_came, up_came, gate_came)
    )
    out_gate = line_result(gate_total, gate_came).astype(F32)
    out_up = line_result(up_total, up_came).astype(F32)

    last_half = line_half(last_sum, last_came)
    last_came = line_mid(last_half)
    query_total = line_total(query_half, query_came)
    query_came = line_out(query_total)
    result = (hidden_in + feed_own + feed_came.astype(F32)).astype(BF16)[None]
    last_came, query_came, result = barrier((last_came, query_came, result))

    last_total = line_total(last_half, last_came)
    last_came = line_out(last_total)
    query_mine = line_result(query_total, query_came)
    query_came = swap_x(query_mine)
    last_came, query_came, out_up, out_gate = barrier(
        (last_came, query_came, out_up, out_gate)
    )
    joined = x_join(query_mine, query_came)
    last_mine = line_result(last_total, last_came)
    last = x_join(last_mine, swap_x(last_mine))
    return (
        result,
        d_inputs[None],
        last[:, 2 * KV_WIDTH],
        last[:, 2 * KV_WIDTH + 1],
        joined[:, output_weight.shape[1] :],
        last[:, :KV_WIDTH],
        last[:, KV_WIDTH : 2 * KV_WIDTH],
        joined[:, : output_weight.shape[1]],
        out_gate,
        out_up,
        out_down,
    )


def solution(mesh):
    return jax.shard_map(
        shards,
        mesh=mesh,
        in_specs=(
            P("shard", ("ctx", "tensor"), None),
            P("shard", ("ctx", "tensor"), None),
            P("shard"),
            P("shard"),
            P("shard", None),
            P("shard", None),
            P("shard", None),
            P("shard", None),
            P("shard", "tensor"),
            P("shard", "tensor"),
            P("tensor", "shard"),
        ),
        out_specs=(
            P("shard", ("ctx", "tensor"), None),
            P("shard", ("ctx", "tensor"), None),
            P("shard"),
            P("shard"),
            P("shard", None),
            P("shard", None),
            P("shard", None),
            P("shard", None),
            P("shard", "tensor"),
            P("shard", "tensor"),
            P("tensor", "shard"),
        ),
        check_vma=False,
    )
```

```python
import functools

import jax
import jax.numpy as jnp
from jax import lax
from jax.experimental import pallas as pl
from jax.experimental.pallas import tpu as pltpu
from jax.sharding import PartitionSpec as P

QUERY_HEADS = 15
SHARED_KV_UNITS = 5
ATTN_UNIT_DIM = 64
GROUP = QUERY_HEADS // SHARED_KV_UNITS
KV_WIDTH = SHARED_KV_UNITS * ATTN_UNIT_DIM
Q_WIDTH = QUERY_HEADS * ATTN_UNIT_DIM

EPS = 1e-05
THETA = 100000.0
F32 = jnp.float32
BF16 = jnp.bfloat16
barrier = lax.optimization_barrier


def rotary_tables(positions):
    half = ATTN_UNIT_DIM // 2
    freqs = THETA ** (-(jnp.arange(half, dtype=F32) * 2.0 / ATTN_UNIT_DIM))
    angles = freqs[:, None] * positions.astype(F32)[None, :]
    return (jnp.cos(angles), jnp.sin(angles))


def rotate(block, cosine, sine):
    split = block.reshape(-1, 2, ATTN_UNIT_DIM // 2, block.shape[1])
    former, latter = split[:, 0], split[:, 1]
    turned = jnp.stack([former * cosine - latter * sine, latter * cosine + former * sine], 1)
    return turned.reshape(block.shape)


def rotate_lanes(block, cosine, sine):
    split = block.reshape(block.shape[0], -1, 2, ATTN_UNIT_DIM // 2)
    former, latter = split[:, :, 0], split[:, :, 1]
    cosine, sine = cosine[:, None, :], sine[:, None, :]
    turned = jnp.stack([former * cosine - latter * sine, latter * cosine + former * sine], 2)
    return turned.reshape(block.shape)


def product(left, right, left_dim, right_dim):
    return lax.dot_general(
        left, right, (((left_dim,), (right_dim,)), ((), ())), preferred_element_type=F32
    )


def swap_core(block):
    size = lax.axis_size("shard")
    return lax.ppermute(block, "shard", [(i, i ^ 1) for i in range(size)])


def shift_y(block, step):
    size = lax.axis_size("shard")
    return lax.ppermute(block, "shard", [(i, (i + 2 * step) % size) for i in range(size)])


def swap_x(block):
    return lax.ppermute(block, "tensor", [(0, 1), (1, 0)])


def shift_z(block, step):
    size = lax.axis_size("ctx")
    pairs = [(i, i + step) for i in range(size) if 0 <= i + step < size]
    return lax.ppermute(block, "ctx", pairs)


def from_other_chips(own):
    return [shift_y(own, -step) for step in range(1, lax.axis_size("shard") // 2)]


def both_cores(held):
    return [piece for block in held for piece in (block, swap_core(block))]


def near_places():
    size = lax.axis_size("shard")
    me = lax.axis_index("shard")
    places = []
    for step in range(size // 2):
        owner = lax.rem(me + 2 * step, size)
        places += [owner, jnp.bitwise_xor(owner, 1)]
    return places


def near_pieces(whole, dim):
    width = whole.shape[dim] // lax.axis_size("shard")
    return [lax.dynamic_slice_in_dim(whole, p * width, width, dim) for p in near_places()]


def in_order(pieces, dim):
    places = near_places()
    ordered = []
    for index in range(len(pieces)):
        piece = pieces[0]
        for place, other in zip(places[1:], pieces[1:]):
            piece = jnp.where(place == index, other, piece)
        ordered.append(piece)
    return jnp.concatenate(ordered, dim)


def add_low(left, right):
    return (left.astype(F32) + right.astype(F32)).astype(BF16)


def block_sums(kept, came):
    return [add_low(kept[step], came[step]) for step in range(kept.shape[0])]


def chip_sends(kept):
    return [shift_y(block, step) for step, block in enumerate(kept) if step > 0]


def chip_sum(kept, came):
    total = kept[0].astype(F32)
    for block in came:
        total = total + block.astype(F32)
    return total.astype(BF16)


def on_line():
    return lax.axis_size("ctx") == 4


def line_in(block):
    return lax.ppermute(block, "ctx", [(0, 1), (3, 2)]) if on_line() else block


def line_mid(half):
    return lax.ppermute(half, "ctx", [(1, 2), (2, 1)]) if on_line() else half


def line_out(total):
    return lax.ppermute(total, "ctx", [(1, 0), (2, 3)]) if on_line() else total


def line_half(block, came):
    return add_low(block, came) if on_line() else lax.psum(block, "ctx")


def line_total(half, came):
    return add_low(half, came) if on_line() else half


def line_result(total, came):
    if not on_line():
        return total
    me = lax.axis_index("ctx")
    return jnp.where(jnp.logical_or(me == 1, me == 2), total, came)


def x_parts(block):
    half = block.shape[0] // 2
    me = lax.axis_index("tensor")
    kept = lax.dynamic_slice_in_dim(block, me * half, half, 0)
    sent = lax.dynamic_slice_in_dim(block, (1 - me) * half, half, 0)
    return kept, sent


def x_join(block, other):
    first = lax.axis_index("tensor") == 0
    return jnp.concatenate(
        [jnp.where(first, block, other), jnp.where(first, other, block)], 0
    ).astype(F32)


def head_part(head, offset=0):
    return slice(offset + head * ATTN_UNIT_DIM, offset + (head + 1) * ATTN_UNIT_DIM)


def causal_mask(keys, lanes, rows):
    key = lax.broadcasted_iota(jnp.int32, (keys, lanes), 0)
    lane = lax.broadcasted_iota(jnp.int32, (keys, lanes), 1)
    return key <= lax.rem(lane, rows)


def forward_first_kernel(query_ref, tile_ref, stats_ref, accum_ref):
    rows = tile_ref.shape[0]
    lanes = query_ref.shape[1]
    mask = causal_mask(rows, lanes, rows)
    stats_ref[...] = jnp.zeros_like(stats_ref)
    for head in range(SHARED_KV_UNITS):
        key = tile_ref[:, head_part(head)]
        value = tile_ref[:, head_part(head, KV_WIDTH)]
        scores = jnp.dot(key, query_ref[head_part(head), :], preferred_element_type=F32)
        scores = jnp.where(mask, scores, -1e30)
        peak = jnp.max(scores, 0, keepdims=True)
        probs = jnp.exp(scores - peak)
        stats_ref[head : head + 1, :] = peak
        stats_ref[8 + head : 9 + head, :] = jnp.sum(probs, 0, keepdims=True)
        accum_ref[head_part(head), :] = product(value, probs.astype(BF16), 0, 0)


def forward_kernel(count, flags_ref, query_ref, *refs):
    tiles, (stats_in, accum_in, stats_ref, accum_ref) = refs[:count], refs[count:]
    stats_ref[...] = stats_in[...]
    accum_ref[...] = accum_in[...]
    for index, tile_ref in enumerate(tiles):

        @pl.when(flags_ref[index] != 0)
        def _(tile_ref=tile_ref):
            for head in range(SHARED_KV_UNITS):
                key = tile_ref[:, head_part(head)]
                value = tile_ref[:, head_part(head, KV_WIDTH)]
                scores = jnp.dot(key, query_ref[head_part(head), :], preferred_element_type=F32)
                old_peak = stats_ref[head : head + 1, :]
                peak = jnp.maximum(old_peak, jnp.max(scores, 0, keepdims=True))
                probs = jnp.exp(scores - peak)
                rescale = jnp.exp(old_peak - peak)
                total = stats_ref[8 + head : 9 + head, :]
                stats_ref[head : head + 1, :] = peak
                stats_ref[8 + head : 9 + head, :] = total * rescale + jnp.sum(
                    probs, 0, keepdims=True
                )
                accum_ref[head_part(head), :] = accum_ref[head_part(head), :] * rescale + (
                    product(value, probs.astype(BF16), 0, 0)
                )


def backward_kernel(causal, count, flags_ref, query_ref, grad_ref, stats_ref, *refs):
    tiles, (into, out_ref), sums = refs[:count], refs[count : count + 2], refs[count + 2 :]
    if len(sums) < count:
        sums = (sums[0], sums[1].at[0], sums[1].at[1])
    rows = tiles[0].shape[0]
    lanes = query_ref.shape[1]
    out_ref[...] = into[...]
    for index, (tile_ref, sum_ref) in enumerate(zip(tiles, sums)):

        @pl.when(flags_ref[index] == 0)
        def _(sum_ref=sum_ref):
            sum_ref[...] = jnp.zeros_like(sum_ref)

        @pl.when(flags_ref[index] != 0)
        def _(tile_ref=tile_ref, sum_ref=sum_ref):
            for head in range(SHARED_KV_UNITS):
                key = tile_ref[:, head_part(head)]
                value = tile_ref[:, head_part(head, KV_WIDTH)]
                query = query_ref[head_part(head), :]
                grad = grad_ref[head_part(head), :]
                scores = jnp.dot(key, query, preferred_element_type=F32)
                probs = jnp.exp(scores - stats_ref[head : head + 1, :])
                if causal:
                    probs = jnp.where(causal_mask(rows, lanes, rows), probs, 0.0)
                d_probs = jnp.dot(value, grad, preferred_element_type=F32)
                d_scores = (probs * (d_probs - stats_ref[8 + head : 9 + head, :])).astype(BF16)
                sum_ref[:, head_part(head)] = product(d_scores, query, 1, 1).astype(BF16)
                sum_ref[:, head_part(head, KV_WIDTH)] = product(
                    probs.astype(BF16), grad, 1, 1
                ).astype(BF16)
                out_ref[head_part(head), :] += product(key, d_scores, 0, 0)


def cost(multiply_adds, values=0, transcendentals=0):
    return pl.CostEstimate(
        flops=2 * multiply_adds, bytes_accessed=values, transcendentals=transcendentals
    )


def tile_cost(count, rows, lanes, matmuls):
    return cost(
        4 * matmuls * count * rows * lanes * KV_WIDTH,
        8 * KV_WIDTH * lanes,
        count * rows * lanes * SHARED_KV_UNITS,
    )


MEMORY = pltpu.CompilerParams(vmem_limit_bytes=24 * 1024 * 1024)
LARGE = pltpu.CompilerParams(vmem_limit_bytes=58 * 1024 * 1024)
IN_VMEM = pl.BlockSpec(memory_space=pltpu.VMEM)
IN_SMEM = pl.BlockSpec(memory_space=pltpu.SMEM)


def on_core(
    kernel, name, out_shape, *operands, estimate, scratch=(), first_in_smem=True, columns=None
):
    def block(shape):
        return pl.BlockSpec(shape, lambda i: (0,) * len(shape))

    specs = [IN_VMEM] * len(operands)
    outs = [IN_VMEM] * len(out_shape)
    if columns is not None:
        last = operands[-1].shape
        specs = [
            block((last[0], columns) if operand.shape == last else operand.shape)
            for operand in operands
        ]
        outs = [block(shape[0]) for shape in out_shape]
    if first_in_smem:
        specs[0] = IN_SMEM
    return pl.pallas_call(
        kernel,
        grid=() if columns is None else (1,),
        in_specs=specs,
        out_specs=tuple(outs),
        out_shape=tuple(jax.ShapeDtypeStruct(*shape) for shape in out_shape),
        scratch_shapes=list(scratch),
        cost_estimate=estimate,
        compiler_params=MEMORY if columns is None else LARGE,
        name=name,
    )(*operands)


def forward_first(query, tile):
    lanes = query.shape[1]
    return on_core(
        forward_first_kernel,
        "attend_own",
        (((16, lanes), F32), ((KV_WIDTH, lanes), F32)),
        query,
        tile,
        estimate=tile_cost(1, tile.shape[0], lanes, 2),
        first_in_smem=False,
    )


def forward_tiles(query, tiles, flags, stats, accum):
    return on_core(
        functools.partial(forward_kernel, len(tiles)),
        "attend",
        ((stats.shape, F32), (accum.shape, F32)),
        jnp.stack(flags).astype(jnp.int32),
        query,
        *tiles,
        stats,
        accum,
        estimate=tile_cost(len(tiles), tiles[0].shape[0], query.shape[1], 2),
    )


def backward_tiles(query, grad, stats, tiles, flags, into, causal=False):
    shape = tiles[0].shape
    sums = (shape, (2,) + shape) if len(tiles) == 3 else (shape,) * len(tiles)
    out = on_core(
        functools.partial(backward_kernel, causal, len(tiles)),
        "attend_back",
        ((into.shape, F32),) + tuple((item, BF16) for item in sums),
        jnp.stack(flags).astype(jnp.int32),
        query,
        grad,
        stats,
        *tiles,
        into,
        estimate=tile_cost(len(tiles), tiles[0].shape[0], query.shape[1], 20),
    )
    return out[0], out[1:]


def to_lanes(block):
    rows = block.shape[1]
    split = block.reshape(SHARED_KV_UNITS, GROUP, ATTN_UNIT_DIM, rows)
    return split.transpose(0, 2, 1, 3).reshape(KV_WIDTH, GROUP * rows)


def place_rows(places, index, width):
    return pl.ds(pl.multiple_of(places[index] * width, 16), width)


def put_in_order(places, pieces, whole, columns, start=0):
    width = pieces[0].shape[0]
    for index, piece in enumerate(pieces):
        whole[place_rows(places, index, width), start : start + columns] = piece[:, :columns]


def mid_kernel(count, places, stats, accum, inputs, gain, *refs):
    weights = refs[:count]
    attended_ref, hidden_ref, normed_ref, weight = refs[count:]
    rows, model = inputs.shape
    put_in_order(places, weights, weight, model)
    for head in range(SHARED_KV_UNITS):
        part = accum[head_part(head), :] / stats[8 + head : 9 + head, :]
        for member in range(GROUP):
            attended_ref[head_part(head * GROUP + member), :] = part[
                :, member * rows : (member + 1) * rows
            ].astype(BF16)
    hidden = inputs[...].astype(F32) + product(attended_ref[...], weight[...], 0, 0)
    hidden_ref[...] = hidden
    inverse = lax.rsqrt(jnp.mean(hidden * hidden, -1, keepdims=True) + EPS)
    normed_ref[:, :model] = (hidden * inverse * gain[...]).astype(BF16)
    normed_ref[:, model:] = jnp.zeros((rows, normed_ref.shape[1] - model), BF16)


def feed_kernel(count, places, *refs):
    normed_own, normed_other, upstream_own, upstream_other = refs[:4]
    gates, ups, downs = (refs[4 + k * count : 4 + (k + 1) * count] for k in range(3))
    units_ref, turned, feed_own, feed_other, grad_own, grad_other = refs[
        4 + 3 * count : 10 + 3 * count
    ]
    gate_up, down, normed, upstream, feed_sum, grad_sum = refs[10 + 3 * count :]
    rows = normed_own.shape[0]
    model, tile = down.shape

    @pl.when(pl.program_id(0) == 0)
    def _():
        normed[:rows, :] = normed_own[...]
        normed[rows:, :] = normed_other[...]
        turned[...] = normed[...].T
        upstream[:rows, :] = upstream_own[...]
        upstream[rows:, :] = upstream_other[...]
        feed_sum[...] = jnp.zeros_like(feed_sum)
        grad_sum[...] = jnp.zeros_like(grad_sum)

    put_in_order(places, gates, gate_up, tile)
    put_in_order(places, ups, gate_up, tile, tile)
    put_in_order(places, downs, down, tile)
    inner = jnp.dot(normed[:, :model], gate_up[...], preferred_element_type=F32)
    gate_val, up_val = inner[:, :tile], inner[:, tile:]
    d_product = jnp.dot(upstream[...], down[...], preferred_element_type=F32)
    sigmoid = 0.5 * jnp.tanh(0.5 * gate_val) + 0.5
    silu = gate_val * sigmoid
    z = (silu * up_val).astype(BF16)
    d_up = (d_product * silu).astype(BF16)
    d_gate = (d_product * up_val * sigmoid * (1.0 + gate_val * (1.0 - sigmoid))).astype(BF16)
    units_ref[:, :tile] = z
    units_ref[:, tile : 2 * tile] = d_gate
    units_ref[:, 2 * tile :] = d_up
    grad_sum[...] += product(units_ref[:, tile:], gate_up[...], 1, 1)
    feed_sum[...] += product(z, down[...], 1, 1)

    @pl.when(pl.program_id(0) == pl.num_programs(0) - 1)
    def _():
        for total, own, other in ((feed_sum, feed_own, feed_other), (grad_sum, grad_own, grad_other)):
            own[...] = total[:rows, :]
            other[...] = total[rows:, :].astype(BF16)


def feed_tile(units):
    return units // 2


def feed_forward(places, rows_in, packed, units):
    count = len(packed)
    rows, wide = rows_in[0].shape
    model = rows_in[2].shape[1]
    width = packed[0].shape[0]
    tile = feed_tile(units)
    steps = units // tile
    whole = pl.BlockSpec((rows, model), lambda i: (0, 0))
    wide_spec = pl.BlockSpec((rows, wide), lambda i: (0, 0))
    gate_spec = pl.BlockSpec((width, tile), lambda i: (0, i))
    up_spec = pl.BlockSpec((width, tile), lambda i: (0, i + steps))
    down_spec = pl.BlockSpec((width, tile), lambda i: (0, i + 2 * steps))
    out_spec = pl.BlockSpec((2 * rows, 3 * tile), lambda i: (0, i))
    return pl.pallas_call(
        functools.partial(feed_kernel, count),
        grid=(steps,),
        in_specs=[IN_SMEM, wide_spec, wide_spec, whole, whole]
        + [gate_spec] * count
        + [up_spec] * count
        + [down_spec] * count,
        out_specs=(out_spec, pl.BlockSpec((wide, 2 * rows), lambda i: (0, 0))) + (whole,) * 4,
        out_shape=(
            jax.ShapeDtypeStruct((2 * rows, 3 * units), BF16),
            jax.ShapeDtypeStruct((wide, 2 * rows), BF16),
        )
        + (
            jax.ShapeDtypeStruct((rows, model), F32),
            jax.ShapeDtypeStruct((rows, model), BF16),
        )
        * 2,
        scratch_shapes=[pltpu.VMEM((model, 2 * tile), BF16), pltpu.VMEM((model, tile), BF16)]
        + [pltpu.VMEM((2 * rows, wide), BF16), pltpu.VMEM((2 * rows, model), BF16)]
        + [pltpu.VMEM((2 * rows, model), F32)] * 2,
        cost_estimate=cost(12 * rows * model * units, 6 * model * units, rows * units),
        compiler_params=LARGE,
        name="feed_forward",
    )(places, *rows_in, *packed, *packed, *packed)


def grad_kernel(count, width, places, turned, values, kept, sent):
    for index in range(count):
        total = jnp.dot(
            turned[place_rows(places, index, width), :], values[...], preferred_element_type=F32
        )
        (kept, sent)[index % 2][index // 2] = total.astype(BF16)


def feed_grads(places, turned, values, units, model, which):
    count = lax.axis_size("shard")
    rows = turned.shape[1]
    width = model // count
    tile = feed_tile(units)
    whole = pl.BlockSpec(turned.shape, lambda i: (0, 0))
    sum_spec = pl.BlockSpec((count // 2, width, tile), lambda i: (0, 0, i))
    return pl.pallas_call(
        functools.partial(grad_kernel, count, width),
        grid=(units // tile,),
        in_specs=[IN_SMEM, whole, pl.BlockSpec((rows, tile), lambda i: (0, 3 * i + which))],
        out_specs=(sum_spec,) * 2,
        out_shape=(jax.ShapeDtypeStruct((count // 2, width, units), BF16),) * 2,
        cost_estimate=cost(2 * rows * model * units, 4 * model * units),
        compiler_params=LARGE,
        name="feed_grads",
    )(places, turned, values)


def turn_kernel(count, places, *refs):
    own, came, hidden_ref, upstream, gain, attended, accum, stats = refs[:8]
    weights = refs[8 : 8 + count]
    d_hidden_ref, grads, stats_ref, kept, sent, gain_ref, turned = refs[8 + count :]
    rows, model = hidden_ref.shape
    width = weights[0].shape[0]
    hidden = hidden_ref[...]
    d_normed = own[...] + came[...].astype(F32)
    inverse = lax.rsqrt(jnp.mean(hidden * hidden, -1, keepdims=True) + EPS)
    gain_ref[...] = jnp.sum(d_normed * hidden * inverse, 0, keepdims=True)
    scaled = d_normed * gain[...]
    d_hidden = (
        upstream[...].astype(F32)
        + inverse * scaled
        - hidden * (inverse * inverse * inverse * jnp.mean(scaled * hidden, -1, keepdims=True))
    )
    d_hidden_ref[...] = d_hidden
    d_branch = d_hidden.astype(BF16)
    for index, weight in enumerate(weights):
        part = place_rows(places, index, width)
        turned[part, :] = product(weight[:, :model], d_branch, 1, 1).astype(BF16)
        (kept, sent)[index % 2][index // 2] = jnp.dot(
            attended[part, :], d_branch, preferred_element_type=F32
        ).astype(BF16)
    stats_ref[...] = jnp.zeros_like(stats_ref)
    for head in range(SHARED_KV_UNITS):
        for member in range(GROUP):
            lanes = slice(member * rows, (member + 1) * rows)
            grads[head_part(head), lanes] = turned[head_part(head * GROUP + member), :]
        total = stats[8 + head : 9 + head, :]
        stats_ref[head : head + 1, :] = stats[head : head + 1, :] + jnp.log(total)
        stats_ref[8 + head : 9 + head, :] = jnp.sum(
            grads[head_part(head), :].astype(F32) * (accum[head_part(head), :] / total),
            0,
            keepdims=True,
        )


def query_kernel(count, places, d_query, cosine, sine, normed, *refs):
    weights = refs[:count]
    kept, sent, d_rows, turned = refs[count:]
    rows = normed.shape[1]
    width = weights[0].shape[0]
    half = ATTN_UNIT_DIM // 2
    scale = ATTN_UNIT_DIM ** (-0.5)
    for head in range(SHARED_KV_UNITS):
        for member in range(GROUP):
            lanes = slice(member * rows, (member + 1) * rows)
            start = head * ATTN_UNIT_DIM
            former = d_query[start : start + half, lanes] * scale
            latter = d_query[start + half : start + 2 * half, lanes] * scale
            start = (head * GROUP + member) * ATTN_UNIT_DIM
            turned[start : start + half, :] = (
                former * cosine[...] + latter * sine[...]
            ).astype(BF16)
            turned[start + half : start + 2 * half, :] = (
                latter * cosine[...] - former * sine[...]
            ).astype(BF16)
    for index, weight in enumerate(weights):
        part = place_rows(places, index, width)
        (kept, sent)[index % 2][index // 2] = product(normed[part, :], turned[...], 1, 1).astype(
            BF16
        )
        d_rows[part, :] = jnp.dot(weight[...], turned[...], preferred_element_type=F32)


def key_kernel(count, places, *refs):
    own, pair, passing, cosine, sine, normed, inputs, inverse, d_query_rows, gain = refs[:10]
    weights = refs[10 : 10 + count]
    kept, sent, d_rows, turned = refs[10 + count :]
    width = normed.shape[0] // count
    half = ATTN_UNIT_DIM // 2
    total = own[...].astype(F32) + pair[...].astype(F32) + passing[...].astype(F32)
    for head in range(SHARED_KV_UNITS):
        start = head * ATTN_UNIT_DIM
        former = total[:, start : start + half]
        latter = total[:, start + half : start + 2 * half]
        turned[:, start : start + half] = (former * cosine[...] + latter * sine[...]).astype(BF16)
        turned[:, start + half : start + 2 * half] = (
            latter * cosine[...] - former * sine[...]
        ).astype(BF16)
    turned[:, KV_WIDTH:] = total[:, KV_WIDTH:].astype(BF16)
    for index, weight in enumerate(weights):
        part = place_rows(places, index, width)
        d_part = d_query_rows[part, :] + product(weight[:width, :], turned[...], 1, 1)
        d_rows[part, :] = d_part
        own_gain = jnp.sum(
            d_part * inputs[part, :].astype(F32) * inverse[...], 1, keepdims=True
        )
        target = (kept, sent)[index % 2]
        target[index // 2, :, : 2 * KV_WIDTH] = jnp.dot(
            normed[part, :], turned[...], preferred_element_type=F32
        ).astype(BF16)
        side = target.shape[2] - 2 * KV_WIDTH
        lane = lax.broadcasted_iota(jnp.int32, (width, side), 1)
        target[index // 2, :, 2 * KV_WIDTH :] = jnp.where(
            lane == 0, own_gain, jnp.where(lane == 1, gain[part, :], 0.0)
        ).astype(BF16)


def shards(
    tokens,
    cotangent,
    prenorm_scaling,
    hidden_gain,
    query_weight,
    key_matrix,
    value_matrix,
    output_weight,
    gate_weight,
    up_weight,
    down_weight,
):
    token_rows = tokens.shape[1]
    units = gate_weight.shape[1]
    ctx_size = lax.axis_size("ctx")
    ctx_me = lax.axis_index("ctx")
    tensor_me = lax.axis_index("tensor")
    scale_factor = ATTN_UNIT_DIM ** (-0.5)
    positions = (ctx_me * 2 + tensor_me) * token_rows + jnp.arange(token_rows, dtype=jnp.int32)
    cosine, sine = rotary_tables(positions)
    inputs = tokens[0].astype(F32)
    unrolled = ctx_size == 4

    gains = jnp.stack([prenorm_scaling, hidden_gain]).astype(BF16)
    own_rows = key_matrix.shape[0]
    own_kv = jnp.concatenate(
        [
            jnp.concatenate([key_matrix, value_matrix], 1),
            jnp.pad(gains, ((0, 14), (0, 2 * KV_WIDTH - own_rows))),
        ],
        0,
    )
    far_kv = from_other_chips(own_kv)
    other_cotangent = swap_x(cotangent[0])
    inv_one = lax.rsqrt(jnp.mean(inputs * inputs, -1, keepdims=True) + EPS)
    far_kv, query_weight, inv_one, tokens_turned = barrier(
        (far_kv, query_weight, inv_one, tokens[0].T)
    )
    far_query = from_other_chips(query_weight)
    kv_pieces = both_cores([own_kv] + far_kv)
    gains = in_order(
        [piece[own_rows : own_rows + 2, :own_rows] for piece in kv_pieces], 1
    ).astype(F32)
    gain_one, gain_two = gains[0], gains[1]
    places = jnp.stack(near_places()).astype(jnp.int32)

    normed_one = (inputs * inv_one * gain_one).astype(BF16)
    normed_one_turned = normed_one.T
    near_one = near_pieces(normed_one, 1)
    projected = sum(
        product(rows, weight[:own_rows], 1, 0) for weight, rows in zip(kv_pieces, near_one)
    )
    key_value = jnp.concatenate(
        [
            rotate_lanes(projected[:, :KV_WIDTH], cosine.T, sine.T).astype(BF16),
            projected[:, KV_WIDTH:].astype(BF16),
        ],
        1,
    )
    far_query, output_weight, other_cotangent, gate_weight = barrier(
        (far_query, output_weight, other_cotangent, gate_weight)
    )
    turned_upstream = jnp.concatenate([cotangent[0], other_cotangent], 0).T
    own_ffn = jnp.concatenate([gate_weight, up_weight, down_weight.T], 1)
    far_output = from_other_chips(output_weight)
    query_pieces = both_cores([query_weight] + far_query)
    query_projected = sum(
        product(weight, rows, 0, 1) for weight, rows in zip(query_pieces, near_one)
    )
    queries = to_lanes((rotate(query_projected, cosine, sine) * scale_factor).astype(BF16))
    later = tensor_me == 1
    flags = [(later if step == 0 else ctx_me >= step) for step in range(ctx_size)]
    passing = key_value
    passing = shift_z(key_value, 1)
    pair_zero = swap_x(key_value)
    stats, accum = forward_first(queries, key_value)
    pair_one, after = swap_x(passing), shift_z(passing, 1)
    stats, accum = forward_tiles(queries, [pair_zero], [flags[0]], stats, accum)
    far_output, own_ffn, stats, pair_one, after = barrier(
        (far_output, own_ffn, stats, pair_one, after)
    )
    far_ffn = from_other_chips(own_ffn)
    tiles = [(key_value, pair_zero), (passing, pair_one), (after, swap_x(after))]
    if unrolled:
        stats, accum = forward_tiles(queries, tiles[1], [flags[1]] * 2, stats, accum)
        after, stats = barrier((shift_z(after, 1), stats))
        tiles.append((after, swap_x(after)))
    for step in range(3, 3 if unrolled else ctx_size):
        after = shift_z(after, 1)
        tiles.append((after, swap_x(after)))
    if unrolled:
        for step in range(2, ctx_size):
            stats, accum = forward_tiles(queries, tiles[step], [flags[step]] * 2, stats, accum)
    else:
        scanned = (
            jnp.stack([tile[0] for tile in tiles[1:]]),
            jnp.stack([tile[1] for tile in tiles[1:]]),
            jnp.stack(flags[1:]),
        )
        (stats, accum), unused = lax.scan(
            lambda held, item: (
                forward_tiles(queries, [item[0], item[1]], [item[2], item[2]], *held),
                None,
            ),
            (stats, accum),
            scanned,
        )

    output_pieces = both_cores([output_weight] + far_output)
    model = tokens.shape[2]
    wide = -(-model // 128) * 128
    attended, hidden_in, normed_two = on_core(
        functools.partial(mid_kernel, len(output_pieces)),
        "attended_to_normed",
        (
            ((Q_WIDTH, token_rows), BF16),
            ((token_rows, model), F32),
            ((token_rows, wide), BF16),
        ),
        places,
        stats,
        accum,
        tokens[0],
        gain_two[None],
        *output_pieces,
        estimate=cost(2 * token_rows * Q_WIDTH * model, 8 * token_rows * model),
        scratch=[pltpu.VMEM((Q_WIDTH, model), BF16)],
        columns=model,
    )
    near_ffn = swap_core(own_ffn)
    normed_two, far_ffn, near_ffn = barrier((normed_two, far_ffn, near_ffn))
    other_normed = swap_x(normed_two)
    ffn_pieces = [own_ffn, near_ffn] + both_cores(far_ffn)
    unit_values, turned, feed_own, feed_other, d_normed_own, d_normed_other = feed_forward(
        places,
        [normed_two, other_normed, cotangent[0], other_cotangent],
        ffn_pieces,
        units,
    )

    d_normed_came = swap_x(d_normed_other)
    kept_down, down_sent = feed_grads(places, turned_upstream, unit_values, units, model, 0)
    kept_gate, gate_sent = feed_grads(places, turned, unit_values, units, model, 1)
    kept_up, up_sent = feed_grads(places, turned, unit_values, units, model, 2)
    down_came = swap_core(down_sent)
    gate_came = swap_core(gate_sent)
    up_came = swap_core(up_sent)

    lanes = queries.shape[1]
    pieces_shape = (len(output_pieces) // 2, query_weight.shape[0])
    d_hidden, grads, stats, output_kept, output_sent, grad_gain_two = on_core(
        functools.partial(turn_kernel, len(output_pieces)),
        "normed_to_attended",
        (
            ((token_rows, model), F32),
            ((KV_WIDTH, lanes), BF16),
            ((16, lanes), F32),
            (pieces_shape + (model,), BF16),
            (pieces_shape + (model,), BF16),
            ((1, model), F32),
        ),
        places,
        d_normed_own,
        d_normed_came,
        hidden_in,
        cotangent[0],
        gain_two[None],
        attended,
        accum,
        stats,
        *output_pieces,
        estimate=cost(40 * token_rows * Q_WIDTH * model, 16 * token_rows * model),
        scratch=[pltpu.VMEM((Q_WIDTH, token_rows), BF16)],
        columns=model,
    )
    output_sent, down_came, gate_came, d_query = barrier(
        (output_sent, down_came, gate_came, jnp.zeros(accum.shape, F32))
    )
    down_kept = block_sums(kept_down, down_came)
    down_came = chip_sends(down_kept)
    gate_kept = block_sums(kept_gate, gate_came)
    gate_came = chip_sends(gate_kept)

    output_came = swap_core(output_sent)
    d_parts = {}
    if unrolled:
        d_query, d_parts[3] = backward_tiles(
            queries, grads, stats, tiles[3], [flags[3]] * 2, d_query
        )
        pair_three = swap_x(d_parts[3][1])
    else:
        d_query, terms = lax.scan(
            lambda held, item: backward_tiles(
                queries, grads, stats, [item[0], item[1]], [item[2], item[2]], held
            ),
            d_query,
            scanned,
        )
        passing = None
        for step in reversed(range(1, ctx_size)):
            part = add_low(terms[0][step - 1], swap_x(terms[1][step - 1]))
            part = part if passing is None else add_low(part, passing)
            passing = shift_z(part, -1)
        pair_three = passing
    down_came, d_query = barrier((down_came, d_query))
    down_sum = chip_sum(down_kept, down_came)
    down_came = line_in(down_sum)
    if unrolled:
        d_query, d_parts[2] = backward_tiles(
            queries, grads, stats, tiles[2], [flags[2]] * 2, d_query
        )
    up_came, output_came, pair_three, d_query = barrier(
        (up_came, output_came, pair_three, d_query)
    )

    up_kept = block_sums(kept_up, up_came)
    up_came = chip_sends(up_kept)
    output_kept = block_sums(output_kept, output_came)
    passing = pair_three
    pair_two = pair_three
    if unrolled:
        pair_two = swap_x(d_parts[2][1])
        passing = shift_z(add_low(d_parts[3][0], pair_three), -1)
        d_query, (own_one, pairs) = backward_tiles(
            queries,
            grads,
            stats,
            [tiles[1][0], tiles[1][1], tiles[0][1]],
            [flags[1], flags[1], flags[0]],
            d_query,
        )
        pair_two, passing, gate_came, down_came, d_query = barrier(
            (pair_two, passing, gate_came, down_came, d_query)
        )
        passing = shift_z(add_low(add_low(d_parts[2][0], pair_two), passing), -1)
    else:
        d_query, (pairs,) = backward_tiles(
            queries, grads, stats, [tiles[0][1]], [flags[0]], d_query
        )
    d_query, (own_zero,) = backward_tiles(
        queries, grads, stats, [key_value], [ctx_me >= 0], d_query, causal=True
    )
    gate_sum = chip_sum(gate_kept, gate_came)
    gate_came = line_in(gate_sum)
    down_half = line_half(down_sum, down_came)
    down_came = line_mid(down_half)
    pairs = swap_x(pairs)
    query_kept, query_sent, d_query_rows = on_core(
        functools.partial(query_kernel, len(query_pieces)),
        "query_grads",
        (
            (pieces_shape + (Q_WIDTH,), BF16),
            (pieces_shape + (Q_WIDTH,), BF16),
            ((model, token_rows), F32),
        ),
        places,
        d_query,
        cosine,
        sine,
        normed_one_turned,
        *query_pieces,
        estimate=cost(4 * token_rows * Q_WIDTH * model, 16 * token_rows * model),
        scratch=[pltpu.VMEM((Q_WIDTH, token_rows), BF16)],
        columns=Q_WIDTH,
    )
    up_came, passing, pairs, query_sent, output_kept = barrier(
        (up_came, passing, pairs, query_sent, output_kept)
    )

    query_came = swap_core(query_sent)
    if unrolled:
        pair_one, pair_zero = pairs[0], pairs[1]
        passing = shift_z(add_low(add_low(own_one, pair_one), passing), -1)
    else:
        pair_zero = pairs
    passing, query_came, down_came, gate_came, d_hidden, grad_gain_two = barrier(
        (passing, query_came, down_came, gate_came, d_hidden, grad_gain_two)
    )

    query_kept = [
        jnp.concatenate([output, query], 1)
        for output, query in zip(output_kept, block_sums(query_kept, query_came))
    ]
    query_came = chip_sends(query_kept)
    gate_half = line_half(gate_sum, gate_came)
    gate_came = line_mid(gate_half)
    up_sum = chip_sum(up_kept, up_came)
    up_came = line_in(up_sum)
    down_total = line_total(down_half, down_came)
    down_came = line_out(down_total)
    last_kept, last_sent, d_rows = on_core(
        functools.partial(key_kernel, len(kv_pieces)),
        "key_value_grads",
        (
            (pieces_shape + (2 * KV_WIDTH + 128,), BF16),
            (pieces_shape + (2 * KV_WIDTH + 128,), BF16),
            ((model, token_rows), F32),
        ),
        places,
        own_zero,
        pair_zero,
        passing,
        cosine.T,
        sine.T,
        normed_one_turned,
        tokens_turned,
        inv_one.T,
        d_query_rows,
        grad_gain_two.T,
        *kv_pieces,
        estimate=cost(4 * token_rows * 2 * KV_WIDTH * model, 16 * token_rows * model),
        scratch=[pltpu.VMEM((token_rows, 2 * KV_WIDTH), BF16)],
        columns=kv_pieces[0].shape[1],
    )
    last_came = swap_core(last_sent)
    query_came, last_came, d_rows, gate_came, up_came = barrier(
        (query_came, last_came, d_rows, gate_came, up_came)
    )

    last_kept = block_sums(last_kept, last_came)
    last_came = chip_sends(last_kept)
    query_mine, query_came = x_parts(chip_sum(query_kept, query_came))
    query_came = swap_x(query_came)
    up_half = line_half(up_sum, up_came)
    up_came = line_mid(up_half)
    gate_total = line_total(gate_half, gate_came)
    gate_came = line_out(gate_total)
    last_came, query_came, up_came, down_came = barrier(
        (last_came, query_came, up_came, down_came)
    )

    last_mine, last_came = x_parts(chip_sum(last_kept, last_came))
    last_came = swap_x(last_came)
    query_sum = add_low(query_mine, query_came)
    query_came = line_in(query_sum)
    up_total = line_total(up_half, up_came)
    up_came = line_out(up_total)
    out_down = line_result(down_total, down_came).T.astype(F32)
    d_normed_one = d_rows.T
    scaled_one = d_normed_one * gain_one
    d_inputs = (
        d_hidden
        + inv_one * scaled_one
        - inputs * inv_one**3 * jnp.mean(scaled_one * inputs, -1, keepdims=True)
    )
    last_came, query_came, d_inputs, out_down = barrier(
        (last_came, query_came, d_inputs, out_down)
    )
    last_sum = add_low(last_mine, last_came)
    last_came = line_in(last_sum)
    query_half = line_half(query_sum, query_came)
    query_came = line_mid(query_half)
    feed_came = swap_x(feed_other)
    last_came, query_came, feed_came, up_came, gate_came = barrier(
        (last_came, query_came, feed_came, up_came, gate_came)
    )
    out_gate = line_result(gate_total, gate_came).astype(F32)
    out_up = line_result(up_total, up_came).astype(F32)

    last_half = line_half(last_sum, last_came)
    last_came = line_mid(last_half)
    query_total = line_total(query_half, query_came)
    query_came = line_out(query_total)
    result = (hidden_in + feed_own + feed_came.astype(F32)).astype(BF16)[None]
    last_came, query_came, result = barrier((last_came, query_came, result))

    last_total = line_total(last_half, last_came)
    last_came = line_out(last_total)
    query_mine = line_result(query_total, query_came)
    query_came = swap_x(query_mine)
    last_came, query_came, out_up, out_gate = barrier(
        (last_came, query_came, out_up, out_gate)
    )
    joined = x_join(query_mine, query_came)
    last_mine = line_result(last_total, last_came)
    last = x_join(last_mine, swap_x(last_mine))
    return (
        result,
        d_inputs[None],
        last[:, 2 * KV_WIDTH],
        last[:, 2 * KV_WIDTH + 1],
        joined[:, output_weight.shape[1] :],
        last[:, :KV_WIDTH],
        last[:, KV_WIDTH : 2 * KV_WIDTH],
        joined[:, : output_weight.shape[1]],
        out_gate,
        out_up,
        out_down,
    )


def solution(mesh):
    return jax.shard_map(
        shards,
        mesh=mesh,
        in_specs=(
            P("shard", ("ctx", "tensor"), None),
            P("shard", ("ctx", "tensor"), None),
            P("shard"),
            P("shard"),
            P("shard", None),
            P("shard", None),
            P("shard", None),
            P("shard", None),
            P("shard", "tensor"),
            P("shard", "tensor"),
            P("tensor", "shard"),
        ),
        out_specs=(
            P("shard", ("ctx", "tensor"), None),
            P("shard", ("ctx", "tensor"), None),
            P("shard"),
            P("shard"),
            P("shard", None),
            P("shard", None),
            P("shard", None),
            P("shard", None),
            P("shard", "tensor"),
            P("shard", "tensor"),
            P("tensor", "shard"),
        ),
        check_vma=False,
    )
```
